256 devices in a mesh: slab: 16 (over z, x_hi), flow: 16 (over y, x_lo, core).
Axes of the slice: x: 4 (x_hi: 2, x_lo: 2; x = x_hi * 2 + x_lo), y: 4, z: 8, core: 2. Of those that a mesh axis runs over, the one named last changes fastest.
Arguments:
- populations: float32 [19, 128, 512, 256], P(None, 'slab', 'flow'), as said below
- offsets: int32 [2], replicated, may hold values from 0 to 511
- fraction: int32 [2], replicated, may hold values from 0 to 63
Outputs:
- advanced: float32 [19, 128, 512, 256], P(None, 'slab', 'flow')
- tallies: float32 [2, 4], replicated
The draws below stay inside these ranges and needn't reach their ends.
Inputs may be any that keep to these rules, and one draw needn't show every extreme that they name: `populations`: every entry is positive.
All inputs are finite; a program needn't handle non-finite values.
Results may differ from the reference program's by a relative error of at most 0.0001.
Values sent between devices are 32-bit elements; how exact they have to be, the bound alone decides.
No kernel may reach another device: no remote copies, remote signals or barrier semaphores. Data moves between devices by JAX's collectives and lax.ppermute only.
A program may use at most 128 MiB of HBM per device.

```python
import jax
import jax.numpy as jnp
import numpy as np

CY = 8
STEPS = 2
DEN = 64
FLOW_CELLS_TOTAL = 512
GRADIENT_ROWS = 128
VORTEX_CELLS = 256
N_SLAB = 16


DRAW_WEIGHTS = np.array([1.0 / 3.0] + [1.0 / 18.0] * 6 + [1.0 / 36.0] * 12, dtype=np.float32)


DRAW_VELOCITY = np.array([[0, 0, 0], [1, 0, 0], [-1, 0, 0], [0, 1, 0], [0, -1, 0], [0, 0, 1], [0, 0, -1], [1, 1, 0], [-1, -1, 0], [1, -1, 0], [-1, 1, 0], [1, 0, 1], [-1, 0, -1], [1, 0, -1], [-1, 0, 1], [0, 1, 1], [0, -1, -1], [0, 1, -1], [0, -1, 1]], dtype=np.float32)


def draw_populations(key, part):
    key = jax.random.fold_in(key, 11)
    height = jnp.arange(GRADIENT_ROWS, dtype=jnp.float32) / max(GRADIENT_ROWS - 1, 1)
    local_density = 2.0 + 4.0 * height
    drift = 0.06 + 0.04 * height
    along_c = DRAW_VELOCITY[:, 0:1] * drift[None, :] + DRAW_VELOCITY[:, 1:2] * 0.04 - DRAW_VELOCITY[:, 2:3] * 0.03
    base = DRAW_WEIGHTS[:, None] * local_density[None, :] * (1.0 + 3.0 * along_c)
    noise = jax.random.uniform(key, (19, GRADIENT_ROWS, FLOW_CELLS_TOTAL, VORTEX_CELLS), jnp.float32, 0.3, 1.7)
    return (base[:, :, None, None] * noise).astype(jnp.float32)


def setup_inputs(seed: int = 0) -> dict:
    key_list = jax.random.split(jax.random.key(seed), 4)
    return {
        "populations": draw_populations(jax.random.fold_in(key_list[3], 71), 0),
        "offsets": jax.random.randint(key_list[1], (STEPS,), 0, FLOW_CELLS_TOTAL).astype(jnp.int32),
        "fraction": jax.random.randint(key_list[2], (STEPS,), 0, DEN).astype(jnp.int32),
    }


WEIGHTS = (1.0 / 3.0,) + (1.0 / 18.0,) * 6 + (1.0 / 36.0,) * 12
VELOCITY = ((0, 0, 0), (1, 0, 0), (-1, 0, 0), (0, 1, 0), (0, -1, 0), (0, 0, 1), (0, 0, -1),
            (1, 1, 0), (-1, -1, 0), (1, -1, 0), (-1, 1, 0), (1, 0, 1), (-1, 0, -1), (1, 0, -1),
            (-1, 0, 1), (0, 1, 1), (0, -1, -1), (0, 1, -1), (0, -1, 1))
RELAXATION = 1.4
SLIDE_SPEED = 0.1


def moments(parts):
    local_density = parts[0]
    for population_count in range(1, 19):
        local_density = local_density + parts[population_count]
    momenta = []
    for component in range(3):
        running = None
        for population_count in range(19):
            factor = VELOCITY[population_count][component]
            if factor == 0:
                continue
            summand = parts[population_count] if factor > 0 else -parts[population_count]
            running = summand if running is None else running + summand
        momenta.append(running)
    return local_density, momenta[0], momenta[1], momenta[2]


def equilibrium(population_count, local_density, velocity_flow, velocity_gradient, velocity_vortex):
    vector = VELOCITY[population_count]
    along_c = vector[0] * velocity_flow + vector[1] * velocity_gradient + vector[2] * velocity_vortex
    squared = velocity_flow * velocity_flow + velocity_gradient * velocity_gradient + velocity_vortex * velocity_vortex
    return WEIGHTS[population_count] * local_density * (1.0 + 3.0 * along_c + 4.5 * along_c * along_c - 1.5 * squared)


def collide(parts, local_density, mom_x, mom_y, mom_z):
    velocity_flow = mom_x / local_density
    velocity_gradient = mom_y / local_density
    velocity_vortex = mom_z / local_density
    post_collision = [parts[population_count] + (equilibrium(population_count, local_density, velocity_flow, velocity_gradient, velocity_vortex) - parts[population_count]) / RELAXATION
               for population_count in range(19)]
    return post_collision, velocity_flow, velocity_gradient, velocity_vortex


def velocity_adjustment(population_count, local_density, velocity_flow, velocity_gradient, velocity_vortex, sliding_sign):
    return (equilibrium(population_count, local_density, velocity_flow + sliding_sign * SLIDE_SPEED, velocity_gradient, velocity_vortex)
            - equilibrium(population_count, local_density, velocity_flow, velocity_gradient, velocity_vortex))


def slab_split(value_grid):
    return value_grid.reshape(N_SLAB, CY, FLOW_CELLS_TOTAL, VORTEX_CELLS)


def advance(parts, local_density, mom_x, mom_y, mom_z, offset, numerator):
    post_collision, velocity_flow, velocity_gradient, velocity_vortex = collide(parts, local_density, mom_x, mom_y, mom_z)
    weight = numerator.astype(jnp.float32) / DEN
    result = []
    for population_count in range(19):
        vector = VELOCITY[population_count]
        incoming_populations = jnp.roll(post_collision[population_count], (vector[1], vector[0], vector[2]), axis=(0, 1, 2))
        if vector[1] != 0:
            if vector[1] == 1:
                border_row, destination_rows, sliding_sign, slab_move = CY - 1, 0, -1.0, 1
            else:
                border_row, destination_rows, sliding_sign, slab_move = 0, CY - 1, 1.0, -1
            slab_border = slab_split(post_collision[population_count])[:, border_row] + velocity_adjustment(
                population_count, slab_split(local_density)[:, border_row], slab_split(velocity_flow)[:, border_row],
                slab_split(velocity_gradient)[:, border_row], slab_split(velocity_vortex)[:, border_row], sliding_sign)
            slab_border = jnp.roll(slab_border, slab_move, axis=0)
            if vector[1] == 1:
                nearer = jnp.roll(slab_border, vector[0] - offset, axis=1)
                farther = jnp.roll(slab_border, vector[0] - offset - 1, axis=1)
            else:
                nearer = jnp.roll(slab_border, vector[0] + offset, axis=1)
                farther = jnp.roll(slab_border, vector[0] + offset + 1, axis=1)
            wall_velocity = (1.0 - weight) * nearer + weight * farther
            wall_velocity = jnp.roll(wall_velocity, vector[2], axis=2)
            incoming_populations = slab_split(incoming_populations).at[:, destination_rows].set(wall_velocity).reshape(GRADIENT_ROWS, FLOW_CELLS_TOTAL, VORTEX_CELLS)
        result.append(incoming_populations)
    return result


def reference(populations, offsets, fraction):
    parts = [populations[population_count] for population_count in range(19)]
    local_density, mom_x, mom_y, mom_z = moments(parts)
    all_cells = FLOW_CELLS_TOTAL * GRADIENT_ROWS * VORTEX_CELLS
    tallies = []
    for section in range(STEPS):
        parts = advance(parts, local_density, mom_x, mom_y, mom_z, offsets[section], fraction[section])
        local_density, mom_x, mom_y, mom_z = moments(parts)
        tallies.append(jnp.stack([jnp.sum(local_density), jnp.sum(mom_x), jnp.sum(mom_y), jnp.sum(mom_z)]) / all_cells)
    return jnp.stack(parts), jnp.stack(tallies)
```

```python
import jax
import jax.numpy as jnp
from jax import lax
from jax.experimental import pallas as pl
from jax.experimental.pallas import tpu as pltpu
from jax.sharding import PartitionSpec as P

STEPS = 2
DEN = 64

VELOCITY = (
    (0, 0, 0),
    (1, 0, 0),
    (-1, 0, 0),
    (0, 1, 0),
    (0, -1, 0),
    (0, 0, 1),
    (0, 0, -1),
    (1, 1, 0),
    (-1, -1, 0),
    (1, -1, 0),
    (-1, 1, 0),
    (1, 0, 1),
    (-1, 0, -1),
    (1, 0, -1),
    (-1, 0, 1),
    (0, 1, 1),
    (0, -1, -1),
    (0, 1, -1),
    (0, -1, 1),
)
WEIGHTS = (1.0 / 3.0,) + (1.0 / 18.0,) * 6 + (1.0 / 36.0,) * 12
OMEGA = 1.0 / 1.4
SLIDE = 0.1
LEVEL = (0, 1, 2, 5, 6, 11, 12, 13, 14)
UPWARD = (3, 7, 10, 15, 17)
DOWNWARD = (4, 8, 9, 16, 18)
RIGHTWARD = (1, 7, 9, 11, 13)
LEFTWARD = (2, 8, 10, 12, 14)
EDGES = UPWARD + DOWNWARD
REACH = 16
HALO = 10 * REACH
EXTRA = HALO + 40
ROWS = EXTRA + 8


def place(n):
    for group, members in enumerate((LEVEL, UPWARD, DOWNWARD)):
        if n in members:
            return group, members.index(n)
    return None


def moments(f):
    diff = [None] + [f[2 * k - 1] - f[2 * k] for k in range(1, 10)]
    rho = f[0]
    for k in range(1, 10):
        rho = rho + (f[2 * k - 1] + f[2 * k])
    m_x = (diff[1] + diff[4]) + (diff[5] + diff[6]) + diff[7]
    m_y = (diff[2] + diff[4]) - (diff[5] - diff[8]) + diff[9]
    m_z = (diff[3] + diff[6]) - (diff[7] - diff[8]) - diff[9]
    return rho, m_x, m_y, m_z


def along(n, u_x, u_y, u_z):
    total = None
    for c, u in zip(VELOCITY[n], (u_x, u_y, u_z)):
        if c:
            term = u if c > 0 else -u
            total = term if total is None else total + term
    return total


def collide(f, rho, m_x, m_y, m_z):
    inverse = 1.0 / rho
    u_x, u_y, u_z = m_x * inverse, m_y * inverse, m_z * inverse
    base = 1.0 - 1.5 * (u_x * u_x + u_y * u_y + u_z * u_z)
    post = [(1.0 - OMEGA) * f[0] + (WEIGHTS[0] * OMEGA) * rho * base]
    for n in range(1, 19, 2):
        scale = (WEIGHTS[n] * OMEGA) * rho
        c_u = along(n, u_x, u_y, u_z)
        even = scale * (base + 4.5 * (c_u * c_u))
        odd = (3.0 * scale) * c_u
        post.append((1.0 - OMEGA) * f[n] + (even + odd))
        post.append((1.0 - OMEGA) * f[n + 1] + (even - odd))
    return post, u_x, u_y, u_z


def wall_change(n, rho, u_x, u_y, u_z, slide):
    c_x = VELOCITY[n][0]
    terms = -3.0 * slide * u_x - 1.5 * slide * slide
    if c_x:
        terms = terms + (
            3.0 * slide * c_x + 4.5 * slide * slide + (9.0 * slide * c_x) * along(n, u_x, u_y, u_z)
        )
    return (WEIGHTS[n] * rho) * terms


def roll_lanes(v, shift):
    return pltpu.roll(v, shift % v.shape[1], axis=1) if shift else v


def store_edges(load, relaxed, side, e_ref, mr_ref, ml_ref, acc_ref):
    members, slide = ((UPWARD, -SLIDE), (DOWNWARD, SLIDE))[side]
    cells = e_ref.shape[1]
    for lo in range(0, cells, 8):
        rows = slice(lo, lo + 8)
        f = load(rows)
        rho, m_x, m_y, m_z = moments(f)
        inverse = 1.0 / rho
        u_x, u_y, u_z = m_x * inverse, m_y * inverse, m_z * inverse
        total = None
        for k, n in enumerate(members):
            j = 5 * side + k
            value = relaxed[k, 0, rows, :] + wall_change(n, rho, u_x, u_y, u_z, slide)
            total = value if total is None else total + value
            e_ref[j, rows, :] = value
            if lo < REACH:
                ml_ref[j * REACH + lo : j * REACH + lo + 8, :] = value
            if lo >= cells - REACH:
                at = j * REACH + lo - (cells - REACH)
                mr_ref[at : at + 8, :] = value
            if VELOCITY[n][0] == 1 and lo == cells - REACH - 8:
                mr_ref[EXTRA + side : EXTRA + side + 1, :] = value[7:8]
            if VELOCITY[n][0] == -1 and lo == REACH:
                ml_ref[EXTRA + side : EXTRA + side + 1, :] = value[0:1]
        if acc_ref is not None:
            acc_ref[5] += (slide / 3.0) * total


def collide_row(y, slab_rows, load, p_refs, e_ref, mr_ref, ml_ref, acc_ref):
    cells = e_ref.shape[1]
    top, bottom = y == slab_rows - 1, y == 0
    for lo in range(0, cells, 8):
        rows = slice(lo, lo + 8)
        f = load(rows)
        rho, m_x, m_y, m_z = moments(f)
        post = collide(f, rho, m_x, m_y, m_z)[0]
        for n in range(19):
            group, k = place(n)
            p_refs[group][k, 0, rows, :] = post[n]
        if acc_ref is not None:
            acc_ref[0] += rho
            acc_ref[1] += m_x
            acc_ref[2] += m_y
            acc_ref[3] += m_z
            edge = jnp.where(bottom, SLIDE, 0.0) - jnp.where(top, SLIDE, 0.0)
            both = jnp.where(bottom | top, SLIDE, 0.0)
            acc_ref[4] += (edge / 6.0) * rho - (both / 2.0) * m_y
            level = sum(post[n] for n in LEVEL[1:]) + post[0]
            up = sum(post[n] for n in UPWARD[1:]) + post[UPWARD[0]]
            down = sum(post[n] for n in DOWNWARD[1:]) + post[DOWNWARD[0]]
            below_top = jnp.where(y == slab_rows - 2, -SLIDE * 2.0 / 3.0, 0.0)
            above_bottom = jnp.where(y == 1, SLIDE * 2.0 / 3.0, 0.0)
            acc_ref[5] += (edge / 6.0) * level + (below_top * up + above_bottom * down)
    for k, n in enumerate(RIGHTWARD):
        group, i = place(n)
        mr_ref[pl.ds(HALO + 8 * k + y, 1), :] = p_refs[group][i, 0, cells - 1 : cells, :]
    for k, n in enumerate(LEFTWARD):
        group, i = place(n)
        ml_ref[pl.ds(HALO + 8 * k + y, 1), :] = p_refs[group][i, 0, 0:1, :]

    @pl.when(top)
    def _():
        store_edges(load, p_refs[1], 0, e_ref, mr_ref, ml_ref, acc_ref)

    @pl.when(bottom)
    def _():
        store_edges(load, p_refs[2], 1, e_ref, mr_ref, ml_ref, acc_ref)


def first_kernel(f_ref, p0, pu, pd, e_ref, mr_ref, ml_ref, t_ref, acc_ref):
    y, slab_rows = pl.program_id(0), pl.num_programs(0)

    @pl.when(y == 0)
    def _():
        acc_ref[...] = jnp.zeros_like(acc_ref)
        mr_ref[EXTRA:ROWS, :] = jnp.zeros((8, mr_ref.shape[1]), jnp.float32)
        ml_ref[EXTRA:ROWS, :] = jnp.zeros((8, ml_ref.shape[1]), jnp.float32)

    def load(rows):
        return [f_ref[n, 0, rows, :] for n in range(19)]

    collide_row(y, slab_rows, load, (p0, pu, pd), e_ref, mr_ref, ml_ref, acc_ref)

    @pl.when(y == slab_rows - 1)
    def _():
        lane = lax.broadcasted_iota(jnp.int32, t_ref.shape, 1)
        out = jnp.zeros(t_ref.shape, jnp.float32)
        for q in range(6):
            out = out + jnp.where(lane == q, jnp.sum(acc_ref[q]), 0.0)
        t_ref[...] = out


def stream_row(y, slab_rows, p0, pu, pd, rl, rr, wu, wd, store):
    cells = p0.shape[2]
    row = lax.broadcasted_iota(jnp.int32, (cells, p0.shape[3]), 0)

    def moved(n):
        group, k = place(n)
        c_x, c_y, c_z = VELOCITY[n]
        v = (p0, pu, pd)[group][k, 0]
        if c_x:
            source = y - c_y
            if c_x == 1:
                halo = rl[pl.ds(HALO + 8 * RIGHTWARD.index(n) + source, 1), :]
                v = jnp.where(row == 0, halo, pltpu.roll(v, 1, axis=0))
            else:
                halo = rr[pl.ds(HALO + 8 * LEFTWARD.index(n) + source, 1), :]
                v = jnp.where(row == cells - 1, halo, pltpu.roll(v, cells - 1, axis=0))
        store(n, roll_lanes(v, c_z))

    for n in LEVEL:
        moved(n)
    for members, walls, at in ((UPWARD, wu, 0), (DOWNWARD, wd, slab_rows - 1)):

        @pl.when(y == at)
        def _(members=members, walls=walls):
            for k, n in enumerate(members):
                store(n, roll_lanes(walls[k], VELOCITY[n][2]))

        @pl.when(y != at)
        def _(members=members):
            for n in members:
                moved(n)


def middle_kernel(
    p0, pu, pd, rl, rr, wu, wd, q0, qu, qd, e_ref, mr_ref, ml_ref, f_ref
):
    y, slab_rows = pl.program_id(0), pl.num_programs(0)

    @pl.when(y == 0)
    def _():
        mr_ref[EXTRA:ROWS, :] = jnp.zeros((8, mr_ref.shape[1]), jnp.float32)
        ml_ref[EXTRA:ROWS, :] = jnp.zeros((8, ml_ref.shape[1]), jnp.float32)

    def store(n, v):
        f_ref[n] = v

    stream_row(y, slab_rows, p0, pu, pd, rl, rr, wu, wd, store)

    def load(rows):
        return [f_ref[n, rows, :] for n in range(19)]

    collide_row(y, slab_rows, load, (q0, qu, qd), e_ref, mr_ref, ml_ref, None)


def last_kernel(p0, pu, pd, rl, rr, wu, wd, o_ref):
    def store(n, v):
        o_ref[n, 0] = v

    stream_row(pl.program_id(0), pl.num_programs(0), p0, pu, pd, rl, rr, wu, wd, store)


def wall_kernel(r_ref, a_ref, e_ref, rl, rr, u_ref, d_ref, s_ref):
    cells = e_ref.shape[1]
    own = REACH + 8
    r, a = r_ref[0], a_ref[0]
    for j, n in enumerate(EDGES):
        side, c_x = j // 5, VELOCITY[n][0]
        s_ref[8:own, :] = rl[j * REACH : (j + 1) * REACH, :]
        s_ref[own : own + cells, :] = e_ref[j]
        s_ref[own + cells : own + cells + REACH, :] = rr[j * REACH : (j + 1) * REACH, :]
        if c_x == 1:
            s_ref[7:8, :] = rl[EXTRA + side : EXTRA + side + 1, :]
        if c_x == -1:
            s_ref[own + cells + REACH : own + cells + REACH + 1, :] = rr[
                EXTRA + side : EXTRA + side + 1, :
            ]
        if side == 0:
            start, out = own - c_x + r, u_ref
            low, high = 1.0 - a, a
        else:
            start, out = own - c_x - r - 1, d_ref
            low, high = a, 1.0 - a
        line = s_ref[...]
        count = line.shape[0]
        line = low * line + high * pltpu.roll(line, count - 1, axis=0)
        out[j % 5] = pltpu.roll(line, count - start, axis=0)[:cells]


def row_spec(count, shape, shift=0):
    last = shape[1] - 1
    return pl.BlockSpec(
        (count, 1, shape[2], shape[3]),
        lambda y: (0, jnp.clip(y + shift, 0, last), 0, 0),
    )


def whole(shape):
    return pl.BlockSpec(shape, lambda y: (0,) * len(shape))


def f32(*shape):
    return jax.ShapeDtypeStruct(shape, jnp.float32)


PARAMS = pltpu.CompilerParams(vmem_limit_bytes=48 * 1024 * 1024)


def local(populations, offsets, fraction):
    _, slab_rows, cells, depth = shape = populations.shape
    slabs, flows = lax.axis_size("slab"), lax.axis_size("flow")
    all_cells = slab_rows * cells * depth * slabs * flows

    split_shapes = tuple(f32(count, slab_rows, cells, depth) for count in (9, 5, 5))
    split_specs = tuple(row_spec(count, shape) for count in (9, 5, 5))
    message = (ROWS, depth)
    edge_shapes = (f32(10, cells, depth), f32(*message), f32(*message))
    edge_specs = (whole((10, cells, depth)), whole(message), whole(message))
    moved_specs = (row_spec(9, shape), row_spec(5, shape, -1), row_spec(5, shape, 1))
    side = (5, cells, depth)
    in_specs = moved_specs + (whole(message), whole(message), whole(side), whole(side))

    def beside(value, distance):
        route = [((i - distance) % flows, i) for i in range(flows)]
        return lax.ppermute(value, "flow", route)

    def displaced(value, slab_step, flow_step):
        route = [
            (((s + slab_step) % slabs) * flows + (f + flow_step) % flows, s * flows + f)
            for s in range(slabs)
            for f in range(flows)
        ]
        return lax.ppermute(value, ("slab", "flow"), route)

    def exchange(section, edges, mr, ml, tally):
        from_left, from_right = beside(mr, 1), beside(ml, -1)
        shift = offsets[section]
        blocks = (shift + REACH) // cells
        rest = (shift - blocks * cells).reshape(1)
        weight = (fraction[section].astype(jnp.float32) / DEN).reshape(1)
        smem = pl.BlockSpec(memory_space=pltpu.SMEM)
        up, down = pl.pallas_call(
            wall_kernel,
            out_shape=(f32(*side), f32(*side)),
            grid=(1,),
            in_specs=[smem, smem, whole((10, cells, depth)), whole(message), whole(message)],
            out_specs=(whole(side), whole(side)),
            scratch_shapes=[pltpu.VMEM((cells + 2 * REACH + 16, depth), jnp.float32)],
            compiler_params=PARAMS,
            name="walls",
        )(rest, weight, edges, from_left, from_right)

        def leaf(blocks_apart):
            def run(up, down, tally):
                from_below = displaced(up, -1, blocks_apart)
                from_above = displaced(down, 1, -blocks_apart)
                axis = ("flow", "slab")[section]
                spread = jnp.broadcast_to(tally[None], (lax.axis_size(axis),) + tally.shape)
                gathered = lax.all_to_all(spread, axis, 0, 0)
                return from_below, from_above, jnp.sum(gathered, axis=0)

            return run

        def twig(first, count):
            def run(up, down, tally):
                return lax.switch(
                    blocks % count,
                    [leaf((first + k) % flows) for k in range(count)],
                    up,
                    down,
                    tally,
                )

            return run

        count = 4
        branches = [twig(first, count) for first in range(0, flows, count)]
        wu, wd, tally = lax.switch((blocks % flows) // count, branches, up, down, tally)
        return from_left, from_right, wu, wd, tally

    p0, pu, pd, edges, mr, ml, tally = pl.pallas_call(
        first_kernel,
        out_shape=split_shapes + edge_shapes + (f32(1, 128),),
        grid=(slab_rows,),
        in_specs=[row_spec(19, shape)],
        out_specs=split_specs + edge_specs + (whole((1, 128)),),
        scratch_shapes=[pltpu.VMEM((6, 8, depth), jnp.float32)],
        compiler_params=PARAMS,
        name="first",
    )(populations)
    from_left, from_right, wu, wd, tally = exchange(0, edges, mr, ml, tally)
    p0, pu, pd, edges, mr, ml = pl.pallas_call(
        middle_kernel,
        out_shape=split_shapes + edge_shapes,
        grid=(slab_rows,),
        in_specs=in_specs,
        out_specs=split_specs + edge_specs,
        scratch_shapes=[pltpu.VMEM((19, cells, depth), jnp.float32)],
        compiler_params=PARAMS,
        name="middle",
    )(p0, pu, pd, from_left, from_right, wu, wd)
    from_left, from_right, wu, wd, tally = exchange(1, edges, mr, ml, tally)
    advanced = pl.pallas_call(
        last_kernel,
        out_shape=f32(*shape),
        grid=(slab_rows,),
        in_specs=in_specs,
        out_specs=row_spec(19, shape),
        compiler_params=PARAMS,
        name="last",
    )(p0, pu, pd, from_left, from_right, wu, wd)

    t = tally[0] / all_cells
    first_x = t[1] + t[4]
    totals = jnp.stack(
        [
            jnp.stack([t[0], first_x, t[2], t[3]]),
            jnp.stack([t[0], first_x + t[5], t[2], t[3]]),
        ]
    )
    return advanced, totals


def solution(mesh):
    in_specs = (P(None, "slab", "flow", None), P(), P())
    out_specs = (P(None, "slab", "flow", None), P())
    return jax.shard_map(local, mesh=mesh, in_specs=in_specs, out_specs=out_specs, check_vma=False)
```

```python
import jax
import jax.numpy as jnp
from jax import lax
from jax.experimental import pallas as pl
from jax.experimental.pallas import tpu as pltpu
from jax.sharding import PartitionSpec as P

STEPS = 2
DEN = 64

VELOCITY = (
    (0, 0, 0),
    (1, 0, 0),
    (-1, 0, 0),
    (0, 1, 0),
    (0, -1, 0),
    (0, 0, 1),
    (0, 0, -1),
    (1, 1, 0),
    (-1, -1, 0),
    (1, -1, 0),
    (-1, 1, 0),
    (1, 0, 1),
    (-1, 0, -1),
    (1, 0, -1),
    (-1, 0, 1),
    (0, 1, 1),
    (0, -1, -1),
    (0, 1, -1),
    (0, -1, 1),
)
WEIGHTS = (1.0 / 3.0,) + (1.0 / 18.0,) * 6 + (1.0 / 36.0,) * 12
OMEGA = 1.0 / 1.4
SLIDE = 0.1
LEVEL = (0, 1, 2, 5, 6, 11, 12, 13, 14)
UPWARD = (3, 7, 10, 15, 17)
DOWNWARD = (4, 8, 9, 16, 18)
RIGHTWARD = (1, 7, 9, 11, 13)
LEFTWARD = (2, 8, 10, 12, 14)
EDGES = UPWARD + DOWNWARD
REACH = 16
HALO = 10 * REACH
EXTRA = HALO + 40
ROWS = EXTRA + 8


def moments(f):
    diff = [None] + [f[2 * k - 1] - f[2 * k] for k in range(1, 10)]
    rho = f[0]
    for k in range(1, 10):
        rho = rho + (f[2 * k - 1] + f[2 * k])
    m_x = (diff[1] + diff[4]) + (diff[5] + diff[6]) + diff[7]
    m_y = (diff[2] + diff[4]) - (diff[5] - diff[8]) + diff[9]
    m_z = (diff[3] + diff[6]) - (diff[7] - diff[8]) - diff[9]
    return rho, m_x, m_y, m_z


def along(n, u_x, u_y, u_z):
    total = None
    for c, u in zip(VELOCITY[n], (u_x, u_y, u_z)):
        if c:
            term = u if c > 0 else -u
            total = term if total is None else total + term
    return total


def collide(f, rho, m_x, m_y, m_z):
    inverse = 1.0 / rho
    u_x, u_y, u_z = m_x * inverse, m_y * inverse, m_z * inverse
    base = 1.0 - 1.5 * (u_x * u_x + u_y * u_y + u_z * u_z)
    post = [(1.0 - OMEGA) * f[0] + (WEIGHTS[0] * OMEGA) * rho * base]
    for n in range(1, 19, 2):
        scale = (WEIGHTS[n] * OMEGA) * rho
        c_u = along(n, u_x, u_y, u_z)
        even = scale * (base + 4.5 * (c_u * c_u))
        odd = (3.0 * scale) * c_u
        post.append((1.0 - OMEGA) * f[n] + (even + odd))
        post.append((1.0 - OMEGA) * f[n + 1] + (even - odd))
    return post, u_x, u_y, u_z


def wall_change(n, rho, u_x, u_y, u_z, slide):
    c_x = VELOCITY[n][0]
    terms = -3.0 * slide * u_x - 1.5 * slide * slide
    if c_x:
        terms = terms + (
            3.0 * slide * c_x + 4.5 * slide * slide + (9.0 * slide * c_x) * along(n, u_x, u_y, u_z)
        )
    return (WEIGHTS[n] * rho) * terms


def roll_lanes(v, shift):
    return pltpu.roll(v, shift % v.shape[1], axis=1) if shift else v


def sum_of(values):
    total = values[0]
    for value in values[1:]:
        total = total + value
    return total


def store_edges(load, p_ref, y, side, e_ref, mr_ref, ml_ref, acc_ref):
    members, slide = ((UPWARD, -SLIDE), (DOWNWARD, SLIDE))[side]
    cells = e_ref.shape[1]
    for lo in range(0, cells, 8):
        rows = slice(lo, lo + 8)
        rho, m_x, m_y, m_z = moments(load(y, lo))
        inverse = 1.0 / rho
        u_x, u_y, u_z = m_x * inverse, m_y * inverse, m_z * inverse
        values = []
        for k, n in enumerate(members):
            j = 5 * side + k
            value = p_ref[n, y, rows, :] + wall_change(n, rho, u_x, u_y, u_z, slide)
            values.append(value)
            e_ref[j, rows, :] = value
            if lo < REACH:
                ml_ref[j * REACH + lo : j * REACH + lo + 8, :] = value
            if lo >= cells - REACH:
                at = j * REACH + lo - (cells - REACH)
                mr_ref[at : at + 8, :] = value
            if VELOCITY[n][0] == 1 and lo == cells - REACH - 8:
                mr_ref[EXTRA + side : EXTRA + side + 1, :] = value[7:8]
            if VELOCITY[n][0] == -1 and lo == REACH:
                ml_ref[EXTRA + side : EXTRA + side + 1, :] = value[0:1]
        if acc_ref is not None:
            acc_ref[5] += (slide / 3.0) * sum_of(values)


def collide_row(y, load, p_ref, mr_ref, ml_ref, acc_ref, slab_rows):
    cells = p_ref.shape[2]
    for lo in range(0, cells, 8):
        rows = slice(lo, lo + 8)
        f = load(y, lo)
        rho, m_x, m_y, m_z = moments(f)
        post = collide(f, rho, m_x, m_y, m_z)[0]
        for n in range(19):
            p_ref[n, y, rows, :] = post[n]
        if acc_ref is not None:
            acc_ref[0] += rho
            acc_ref[1] += m_x
            acc_ref[2] += m_y
            acc_ref[3] += m_z
            top, bottom = y == slab_rows - 1, y == 0
            edge = jnp.where(bottom, SLIDE, 0.0) - jnp.where(top, SLIDE, 0.0)
            both = jnp.where(bottom | top, SLIDE, 0.0)
            acc_ref[4] += (edge / 6.0) * rho - (both / 2.0) * m_y
            level, up, down = (sum_of([post[n] for n in ns]) for ns in (LEVEL, UPWARD, DOWNWARD))
            below_top = jnp.where(y == slab_rows - 2, -SLIDE * 2.0 / 3.0, 0.0)
            above_bottom = jnp.where(y == 1, SLIDE * 2.0 / 3.0, 0.0)
            acc_ref[5] += (edge / 6.0) * level + (below_top * up + above_bottom * down)
    for k, n in enumerate(RIGHTWARD):
        mr_ref[pl.ds(HALO + 8 * k + y, 1), :] = p_ref[n, y, cells - 1 : cells, :]
    for k, n in enumerate(LEFTWARD):
        ml_ref[pl.ds(HALO + 8 * k + y, 1), :] = p_ref[n, y, 0:1, :]


def clear_rest(*messages):
    for message in messages:
        message[EXTRA:ROWS, :] = jnp.zeros((ROWS - EXTRA, message.shape[1]), jnp.float32)


def first_kernel(f_hbm, p_hbm, e_ref, mr_ref, ml_ref, t_ref, f_ref, p_ref, acc_ref, in_sems, out_sems):
    slab_rows = f_ref.shape[1]

    def arriving(y):
        return pltpu.make_async_copy(f_hbm.at[:, y], f_ref.at[:, y], in_sems.at[y])

    def leaving(y):
        return pltpu.make_async_copy(p_ref.at[:, y], p_hbm.at[:, y], out_sems.at[y])

    for y in range(slab_rows):
        arriving(y).start()
    acc_ref[...] = jnp.zeros_like(acc_ref)
    clear_rest(mr_ref, ml_ref)

    def load(y, lo):
        return [f_ref[n, y, lo : lo + 8, :] for n in range(19)]

    def step(y, carry):
        arriving(y).wait()
        collide_row(y, load, p_ref, mr_ref, ml_ref, acc_ref, slab_rows)
        leaving(y).start()
        return carry

    lax.fori_loop(0, slab_rows, step, 0)
    store_edges(load, p_ref, slab_rows - 1, 0, e_ref, mr_ref, ml_ref, acc_ref)
    store_edges(load, p_ref, 0, 1, e_ref, mr_ref, ml_ref, acc_ref)
    lane = lax.broadcasted_iota(jnp.int32, t_ref.shape, 2)
    out = jnp.zeros(t_ref.shape, jnp.float32)
    for q in range(6):
        out = out + jnp.where(lane == q, jnp.sum(acc_ref[q]), 0.0)
    t_ref[...] = out
    for y in range(slab_rows):
        leaving(y).wait()


def streamed(p_ref, rl, rr, wu, wd, slab_rows):
    cells = p_ref.shape[2]
    row = lax.broadcasted_iota(jnp.int32, (8, p_ref.shape[3]), 0)

    def load(y, lo):
        out = []
        for n, (c_x, c_y, c_z) in enumerate(VELOCITY):
            if c_y == 1 and isinstance(y, int) and y == 0:
                v = wu[UPWARD.index(n), lo : lo + 8, :]
            elif c_y == -1 and isinstance(y, int) and y == slab_rows - 1:
                v = wd[DOWNWARD.index(n), lo : lo + 8, :]
            elif c_x == 1 and lo == 0:
                halo = rl[pl.ds(HALO + 8 * RIGHTWARD.index(n) + y - c_y, 1), :]
                v = jnp.where(row == 0, halo, pltpu.roll(p_ref[n, y - c_y, 0:8, :], 1, axis=0))
            elif c_x == -1 and lo == cells - 8:
                halo = rr[pl.ds(HALO + 8 * LEFTWARD.index(n) + y - c_y, 1), :]
                v = jnp.where(
                    row == 7, halo, pltpu.roll(p_ref[n, y - c_y, cells - 8 : cells, :], 7, axis=0)
                )
            else:
                v = p_ref[n, y - c_y, lo - c_x : lo - c_x + 8, :]
            out.append(roll_lanes(v, c_z))
        return out

    return load


def next_kernel(
    all_cells,
    step_ref,
    p_hbm,
    rl,
    rr,
    wu,
    wd,
    g_ref,
    o_hbm,
    e_ref,
    mr_ref,
    ml_ref,
    s_ref,
    p_ref,
    q_ref,
    in_sems,
    out_sems,
):
    slab_rows, cells = p_ref.shape[1:3]

    def arriving(y):
        return pltpu.make_async_copy(p_hbm.at[:, y], p_ref.at[:, y], in_sems.at[y])

    def leaving(y):
        return pltpu.make_async_copy(q_ref.at[:, y], o_hbm.at[:, y], out_sems.at[y])

    for y in range(slab_rows):
        arriving(y).start()
    clear_rest(mr_ref, ml_ref)
    total = g_ref[0] * (1.0 / all_cells)
    lane = lax.broadcasted_iota(jnp.int32, total.shape, 1)
    rho, m_x, m_y, m_z, first, second = (
        jnp.sum(jnp.where(lane == q, total, 0.0)) for q in range(6)
    )
    at = lax.broadcasted_iota(jnp.int32, s_ref.shape, 1)
    x = m_x + first + jnp.where(lax.broadcasted_iota(jnp.int32, s_ref.shape, 0) == 1, second, 0.0)
    s_ref[...] = jnp.where(at == 0, rho, jnp.where(at == 1, x, jnp.where(at == 2, m_y, m_z)))

    load = streamed(p_ref, rl, rr, wu, wd, slab_rows)

    def all_rows(work):
        def step(y, carry):
            arriving(y + 1).wait()
            work(y)
            leaving(y).start()
            return carry

        arriving(0).wait()
        step(0, 0)
        lax.fori_loop(1, slab_rows - 1, step, 0)
        work(slab_rows - 1)
        leaving(slab_rows - 1).start()

    def store(y):
        for lo in range(0, cells, 8):
            for n, v in enumerate(load(y, lo)):
                q_ref[n, y, lo : lo + 8, :] = v

    @pl.when(step_ref[0] < STEPS - 1)
    def _():
        all_rows(lambda y: collide_row(y, load, q_ref, mr_ref, ml_ref, None, slab_rows))
        store_edges(load, q_ref, slab_rows - 1, 0, e_ref, mr_ref, ml_ref, None)
        store_edges(load, q_ref, 0, 1, e_ref, mr_ref, ml_ref, None)

    @pl.when(step_ref[0] == STEPS - 1)
    def _():
        all_rows(store)

    for y in range(slab_rows):
        leaving(y).wait()


def wall_kernel(step_ref, d_ref, n_ref, g_ref, e_ref, rl, rr, up_ref, down_ref, t_ref, s_ref):
    cells = e_ref.shape[1]
    own = REACH + 8
    section = step_ref[0]
    r = lax.rem(d_ref[section] + REACH, cells) - REACH
    a = n_ref[section].astype(jnp.float32) * (1.0 / DEN)
    t_ref[...] = jnp.broadcast_to(jnp.sum(g_ref[...], axis=0, keepdims=True), t_ref.shape)
    for j, n in enumerate(EDGES):
        side, c_x = j // 5, VELOCITY[n][0]
        s_ref[8:own, :] = rl[j * REACH : (j + 1) * REACH, :]
        s_ref[own : own + cells, :] = e_ref[j]
        s_ref[own + cells : own + cells + REACH, :] = rr[j * REACH : (j + 1) * REACH, :]
        if c_x == 1:
            s_ref[7:8, :] = rl[EXTRA + side : EXTRA + side + 1, :]
        if c_x == -1:
            s_ref[own + cells + REACH : own + cells + REACH + 1, :] = rr[
                EXTRA + side : EXTRA + side + 1, :
            ]
        if side == 0:
            start, out = own - c_x + r, up_ref
            low, high = 1.0 - a, a
        else:
            start, out = own - c_x - r - 1, down_ref
            low, high = a, 1.0 - a
        line = s_ref[...]
        count = line.shape[0]
        line = low * line + high * pltpu.roll(line, count - 1, axis=0)
        out[j % 5] = pltpu.roll(line, count - start, axis=0)[:cells]


VMEM = pl.BlockSpec(memory_space=pltpu.VMEM)
SMEM = pl.BlockSpec(memory_space=pltpu.SMEM)
HBM = pl.BlockSpec(memory_space=pltpu.HBM)
PARAMS = pltpu.CompilerParams(vmem_limit_bytes=24 * 1024 * 1024)


def near(*shape):
    return pltpu.VMEM(shape, jnp.float32)


def kept(*values):
    return tuple(pltpu.with_memory_space_constraint(v, pltpu.VMEM) for v in values)


def local(populations, offsets, fraction):
    _, slab_rows, cells, depth = shape = populations.shape
    slabs, flows = lax.axis_size("slab"), lax.axis_size("flow")
    all_cells = slab_rows * cells * depth * slabs * flows
    side = (5, cells, depth)
    both = ("slab", "flow")
    everyone = [(s, f) for s in range(slabs) for f in range(flows)]

    def beside(value, distance):
        route = [((i - distance) % flows, i) for i in range(flows)]
        return lax.ppermute(value, "flow", route)

    def displaced(value, slab_step, flow_step):
        route = [
            (((s + slab_step) % slabs) * flows + (f + flow_step) % flows, s * flows + f)
            for s, f in everyone
        ]
        return lax.ppermute(value, both, route)

    state = pltpu.HBM(shape, jnp.float32)
    edge_outs = (
        near(10, cells, depth),
        near(ROWS, depth),
        near(ROWS, depth),
    )
    buffers = [pltpu.VMEM(shape, jnp.float32)] * 2
    row_sems = [pltpu.SemaphoreType.DMA((slab_rows,))] * 2

    first = pl.pallas_call(
        first_kernel,
        out_shape=(state,) + edge_outs + (near(flows, 1, 128),),
        in_specs=[HBM],
        out_specs=(HBM,) + (VMEM,) * 4,
        scratch_shapes=buffers + [pltpu.VMEM((6, 8, depth), jnp.float32)] + row_sems,
        compiler_params=PARAMS,
        name="first",
    )
    walls = pl.pallas_call(
        wall_kernel,
        out_shape=(near(*side), near(*side), near(slabs, 1, 128)),
        in_specs=[SMEM] * 3 + [VMEM] * 4,
        out_specs=(VMEM,) * 3,
        scratch_shapes=[pltpu.VMEM((cells + 2 * REACH + 16, depth), jnp.float32)],
        compiler_params=PARAMS,
        name="walls",
    )
    following = pl.pallas_call(
        lambda *refs: next_kernel(all_cells, *refs),
        out_shape=(state,) + edge_outs + (near(STEPS, 4),),
        in_specs=[SMEM, HBM] + [VMEM] * 5,
        out_specs=(HBM,) + (VMEM,) * 4,
        scratch_shapes=buffers + row_sems,
        input_output_aliases={1: 0},
        compiler_params=PARAMS,
        name="following",
    )

    def leaf(blocks_apart):
        return lambda up, down: (
            displaced(up, -1, blocks_apart),
            displaced(down, 1, -blocks_apart),
        )

    def twig(start, count):
        leaves = [leaf(start + k) for k in range(count)]
        return lambda inner, up, down: lax.switch(inner, leaves, up, down)

    count = 4
    branches = [twig(start, count) for start in range(0, flows, count)]
    blocks = [((offsets[k] + REACH) // cells) % flows for k in range(STEPS)]

    def neighbours(axis, mr, ml, sums):
        from_left, from_right = beside(mr, 1), beside(ml, -1)
        return from_left, from_right, lax.all_to_all(sums, axis, 0, 0)

    def step(section, carry):
        p, edges, from_left, from_right, gathered, _, now, *later = carry
        at = section.reshape(1)
        up, down, sums = walls(
            at, offsets, fraction, *kept(gathered, edges, from_left, from_right)
        )
        wu, wd = lax.switch(now // count, branches, now % count, up, down)
        p, edges, mr, ml, totals = following(
            at,
            pltpu.with_memory_space_constraint(p, pltpu.HBM),
            *kept(from_left, from_right, wu, wd, sums),
        )
        from_left, from_right, gathered = lax.cond(
            section < STEPS - 1,
            lambda mr, ml, sums: neighbours("slab", mr, ml, sums),
            lambda mr, ml, sums: (mr, ml, sums),
            mr,
            ml,
            sums,
        )
        return p, edges, from_left, from_right, gathered, totals, *later, now

    p, edges, mr, ml, sums = first(pltpu.with_memory_space_constraint(populations, pltpu.HBM))
    from_left, from_right, gathered = neighbours("flow", mr, ml, sums)
    totals = jnp.zeros((STEPS, 4), jnp.float32)
    carry = (p, edges, from_left, from_right, gathered, totals, *blocks)
    carry = lax.fori_loop(0, STEPS, step, carry)
    return carry[0], carry[5]


def solution(mesh):
    in_specs = (P(None, "slab", "flow", None), P(), P())
    out_specs = (P(None, "slab", "flow", None), P())
    return jax.shard_map(local, mesh=mesh, in_specs=in_specs, out_specs=out_specs, check_vma=False)
```

```python
import jax
import jax.numpy as jnp
from jax import lax
from jax.experimental import pallas as pl
from jax.experimental.pallas import tpu as pltpu
from jax.sharding import PartitionSpec as P

STEPS = 2
DEN = 64

VELOCITY = (
    (0, 0, 0),
    (1, 0, 0),
    (-1, 0, 0),
    (0, 1, 0),
    (0, -1, 0),
    (0, 0, 1),
    (0, 0, -1),
    (1, 1, 0),
    (-1, -1, 0),
    (1, -1, 0),
    (-1, 1, 0),
    (1, 0, 1),
    (-1, 0, -1),
    (1, 0, -1),
    (-1, 0, 1),
    (0, 1, 1),
    (0, -1, -1),
    (0, 1, -1),
    (0, -1, 1),
)
WEIGHTS = (1.0 / 3.0,) + (1.0 / 18.0,) * 6 + (1.0 / 36.0,) * 12
OMEGA = 1.0 / 1.4
SLIDE = 0.1
LEVEL = (0, 1, 2, 5, 6, 11, 12, 13, 14)
UPWARD = (3, 7, 10, 15, 17)
DOWNWARD = (4, 8, 9, 16, 18)
RIGHTWARD = (1, 7, 9, 11, 13)
LEFTWARD = (2, 8, 10, 12, 14)
EDGES = UPWARD + DOWNWARD
REACH = 16
HALO = 10 * REACH
EXTRA = HALO + 40
ROWS = EXTRA + 8
STRIDE = 4


def moments(f):
    diff = [None] + [f[2 * k - 1] - f[2 * k] for k in range(1, 10)]
    rho = f[0]
    for k in range(1, 10):
        rho = rho + (f[2 * k - 1] + f[2 * k])
    m_x = (diff[1] + diff[4]) + (diff[5] + diff[6]) + diff[7]
    m_y = (diff[2] + diff[4]) - (diff[5] - diff[8]) + diff[9]
    m_z = (diff[3] + diff[6]) - (diff[7] - diff[8]) - diff[9]
    return rho, m_x, m_y, m_z


def along(n, u_x, u_y, u_z):
    total = None
    for c, u in zip(VELOCITY[n], (u_x, u_y, u_z)):
        if c:
            term = u if c > 0 else -u
            total = term if total is None else total + term
    return total


def collide(f, rho, m_x, m_y, m_z):
    inverse = 1.0 / rho
    u_x, u_y, u_z = m_x * inverse, m_y * inverse, m_z * inverse
    base = 1.0 - 1.5 * (u_x * u_x + u_y * u_y + u_z * u_z)
    post = [(1.0 - OMEGA) * f[0] + (WEIGHTS[0] * OMEGA) * rho * base]
    for n in range(1, 19, 2):
        scale = (WEIGHTS[n] * OMEGA) * rho
        c_u = along(n, u_x, u_y, u_z)
        even = scale * (base + 4.5 * (c_u * c_u))
        odd = (3.0 * scale) * c_u
        post.append((1.0 - OMEGA) * f[n] + (even + odd))
        post.append((1.0 - OMEGA) * f[n + 1] + (even - odd))
    return post, u_x, u_y, u_z


def wall_change(n, rho, u_x, u_y, u_z, slide):
    c_x = VELOCITY[n][0]
    terms = -3.0 * slide * u_x - 1.5 * slide * slide
    if c_x:
        terms = terms + (
            3.0 * slide * c_x + 4.5 * slide * slide + (9.0 * slide * c_x) * along(n, u_x, u_y, u_z)
        )
    return (WEIGHTS[n] * rho) * terms


def roll_lanes(v, shift):
    return pltpu.roll(v, shift % v.shape[1], axis=1) if shift else v


def sum_of(values):
    total = values[0]
    for value in values[1:]:
        total = total + value
    return total


def store_edges(load, p_ref, y, side, e_ref, mr_ref, ml_ref, acc_ref):
    members, slide = ((UPWARD, -SLIDE), (DOWNWARD, SLIDE))[side]
    cells = e_ref.shape[1]
    for lo in range(0, cells, 8):
        rows = slice(lo, lo + 8)
        rho, m_x, m_y, m_z = moments(load(y, lo))
        inverse = 1.0 / rho
        u_x, u_y, u_z = m_x * inverse, m_y * inverse, m_z * inverse
        values = []
        for k, n in enumerate(members):
            j = 5 * side + k
            value = p_ref[n, y, rows, :] + wall_change(n, rho, u_x, u_y, u_z, slide)
            values.append(value)
            e_ref[j, rows, :] = value
            if lo < REACH:
                ml_ref[j * REACH + lo : j * REACH + lo + 8, :] = value
            if lo >= cells - REACH:
                at = j * REACH + lo - (cells - REACH)
                mr_ref[at : at + 8, :] = value
            if VELOCITY[n][0] == 1 and lo == cells - REACH - 8:
                mr_ref[EXTRA + side : EXTRA + side + 1, :] = value[7:8]
            if VELOCITY[n][0] == -1 and lo == REACH:
                ml_ref[EXTRA + side : EXTRA + side + 1, :] = value[0:1]
        if acc_ref is not None:
            acc_ref[5] += (slide / 3.0) * sum_of(values)


def collide_row(y, load, p_ref, mr_ref, ml_ref, acc_ref, slab_rows):
    cells = p_ref.shape[2]
    for lo in range(0, cells, 8):
        rows = slice(lo, lo + 8)
        f = load(y, lo)
        rho, m_x, m_y, m_z = moments(f)
        post = collide(f, rho, m_x, m_y, m_z)[0]
        for n in range(19):
            p_ref[n, y, rows, :] = post[n]
        if acc_ref is not None:
            acc_ref[0] += rho
            acc_ref[1] += m_x
            acc_ref[2] += m_y
            acc_ref[3] += m_z
            top, bottom = y == slab_rows - 1, y == 0
            edge = jnp.where(bottom, SLIDE, 0.0) - jnp.where(top, SLIDE, 0.0)
            both = jnp.where(bottom | top, SLIDE, 0.0)
            acc_ref[4] += (edge / 6.0) * rho - (both / 2.0) * m_y
            level, up, down = (sum_of([post[n] for n in ns]) for ns in (LEVEL, UPWARD, DOWNWARD))
            below_top = jnp.where(y == slab_rows - 2, -SLIDE * 2.0 / 3.0, 0.0)
            above_bottom = jnp.where(y == 1, SLIDE * 2.0 / 3.0, 0.0)
            acc_ref[5] += (edge / 6.0) * level + (below_top * up + above_bottom * down)
    for k, n in enumerate(RIGHTWARD):
        mr_ref[pl.ds(HALO + 8 * k + y, 1), :] = p_ref[n, y, cells - 1 : cells, :]
    for k, n in enumerate(LEFTWARD):
        ml_ref[pl.ds(HALO + 8 * k + y, 1), :] = p_ref[n, y, 0:1, :]


def clear_rest(*messages):
    for message in messages:
        message[EXTRA:ROWS, :] = jnp.zeros((ROWS - EXTRA, message.shape[1]), jnp.float32)


def first_kernel(
    f_hbm,
    p_hbm,
    e_ref,
    mr_ref,
    ml_ref,
    t_ref,
    t0_ref,
    t1_ref,
    t2_ref,
    t3_ref,
    f_ref,
    p_ref,
    acc_ref,
    in_sems,
    out_sems,
):
    slab_rows = f_ref.shape[1]

    def arriving(y):
        return pltpu.make_async_copy(f_hbm.at[:, y], f_ref.at[:, y], in_sems.at[y])

    def leaving(y):
        return pltpu.make_async_copy(p_ref.at[:, y], p_hbm.at[:, y], out_sems.at[y])

    for y in range(slab_rows):
        arriving(y).start()
    acc_ref[...] = jnp.zeros_like(acc_ref)
    clear_rest(mr_ref, ml_ref)
    for table in (t0_ref, t1_ref, t2_ref, t3_ref):
        table[...] = jnp.zeros_like(table)

    def load(y, lo):
        return [f_ref[n, y, lo : lo + 8, :] for n in range(19)]

    def step(y, carry):
        arriving(y).wait()
        collide_row(y, load, p_ref, mr_ref, ml_ref, acc_ref, slab_rows)
        leaving(y).start()
        return carry

    lax.fori_loop(0, slab_rows, step, 0)
    store_edges(load, p_ref, slab_rows - 1, 0, e_ref, mr_ref, ml_ref, acc_ref)
    store_edges(load, p_ref, 0, 1, e_ref, mr_ref, ml_ref, acc_ref)
    lane = lax.broadcasted_iota(jnp.int32, t_ref.shape, 2)
    out = jnp.zeros(t_ref.shape, jnp.float32)
    for q in range(6):
        out = out + jnp.where(lane == q, jnp.sum(acc_ref[q]), 0.0)
    t_ref[...] = out
    for y in range(slab_rows):
        leaving(y).wait()


def streamed(p_ref, rl, rr, wu, wd, slab_rows):
    cells = p_ref.shape[2]
    row = lax.broadcasted_iota(jnp.int32, (8, p_ref.shape[3]), 0)

    def load(y, lo):
        out = []
        for n, (c_x, c_y, c_z) in enumerate(VELOCITY):
            if c_y == 1 and isinstance(y, int) and y == 0:
                v = wu[UPWARD.index(n) * cells + lo : UPWARD.index(n) * cells + lo + 8, :]
            elif c_y == -1 and isinstance(y, int) and y == slab_rows - 1:
                v = wd[DOWNWARD.index(n) * cells + lo : DOWNWARD.index(n) * cells + lo + 8, :]
            elif c_x == 1 and lo == 0:
                halo = rl[pl.ds(HALO + 8 * RIGHTWARD.index(n) + y - c_y, 1), :]
                v = jnp.where(row == 0, halo, pltpu.roll(p_ref[n, y - c_y, 0:8, :], 1, axis=0))
            elif c_x == -1 and lo == cells - 8:
                halo = rr[pl.ds(HALO + 8 * LEFTWARD.index(n) + y - c_y, 1), :]
                v = jnp.where(
                    row == 7, halo, pltpu.roll(p_ref[n, y - c_y, cells - 8 : cells, :], 7, axis=0)
                )
            else:
                v = p_ref[n, y - c_y, lo - c_x : lo - c_x + 8, :]
            out.append(roll_lanes(v, c_z))
        return out

    return load


def next_kernel(
    all_cells,
    step_ref,
    slab_ref,
    p_hbm,
    rl,
    rr,
    wu,
    wd,
    up_ref,
    o_hbm,
    e_ref,
    mr_ref,
    ml_ref,
    t_ref,
    s_ref,
    p_ref,
    q_ref,
    in_sems,
    out_sems,
):
    slab_rows, cells = p_ref.shape[1:3]

    def arriving(y):
        return pltpu.make_async_copy(p_hbm.at[:, y], p_ref.at[:, y], in_sems.at[y])

    def leaving(y):
        return pltpu.make_async_copy(q_ref.at[:, y], o_hbm.at[:, y], out_sems.at[y])

    for y in range(slab_rows):
        arriving(y).start()
    clear_rest(mr_ref, ml_ref)
    known, below, above = (ref[5 * cells :, :] for ref in (up_ref, wu, wd))
    t_ref[...] = known + below + above
    ahead = (slab_rows_of(known.shape) - slab_ref[0]) & (STRIDE - 1)
    total = jnp.sum(jnp.where(ahead == 2, above, known), axis=0, keepdims=True)
    total = (total[:, :128] + total[:, 128:]) * (1.0 / all_cells)
    lane = lax.broadcasted_iota(jnp.int32, total.shape, 1)
    rho, m_x, m_y, m_z, first, second = (
        jnp.sum(jnp.where(lane == q, total, 0.0)) for q in range(6)
    )
    at = lax.broadcasted_iota(jnp.int32, s_ref.shape, 1)
    x = m_x + first + jnp.where(lax.broadcasted_iota(jnp.int32, s_ref.shape, 0) == 1, second, 0.0)
    s_ref[...] = jnp.where(at == 0, rho, jnp.where(at == 1, x, jnp.where(at == 2, m_y, m_z)))

    load = streamed(p_ref, rl, rr, wu, wd, slab_rows)

    def all_rows(work):
        def step(y, carry):
            arriving(y + 1).wait()
            work(y)
            leaving(y).start()
            return carry

        arriving(0).wait()
        step(0, 0)
        lax.fori_loop(1, slab_rows - 1, step, 0)
        work(slab_rows - 1)
        leaving(slab_rows - 1).start()

    def store(y):
        for lo in range(0, cells, 8):
            for n, v in enumerate(load(y, lo)):
                q_ref[n, y, lo : lo + 8, :] = v

    @pl.when(step_ref[0] < STEPS - 1)
    def _():
        all_rows(lambda y: collide_row(y, load, q_ref, mr_ref, ml_ref, None, slab_rows))
        store_edges(load, q_ref, slab_rows - 1, 0, e_ref, mr_ref, ml_ref, None)
        store_edges(load, q_ref, 0, 1, e_ref, mr_ref, ml_ref, None)

    @pl.when(step_ref[0] == STEPS - 1)
    def _():
        all_rows(store)

    for y in range(slab_rows):
        leaving(y).wait()


def slab_rows_of(shape):
    half = jnp.where(lax.broadcasted_iota(jnp.int32, shape, 1) >= shape[1] // 2, 1, 0)
    return lax.broadcasted_iota(jnp.int32, shape, 0) + shape[0] * half


def wall_kernel(
    step_ref,
    slab_ref,
    d_ref,
    n_ref,
    g_ref,
    own_ref,
    t1_ref,
    t2_ref,
    t3_ref,
    e_ref,
    rl,
    rr,
    up_ref,
    down_ref,
    s_ref,
):
    cells = e_ref.shape[1]
    own = REACH + 8
    section = step_ref[0]
    r = lax.rem(d_ref[section] + REACH, cells) - REACH
    a = n_ref[section].astype(jnp.float32) * (1.0 / DEN)
    local = jnp.sum(g_ref[...], axis=0)
    local = jnp.broadcast_to(jnp.concatenate([local, local], axis=1), own_ref.shape)
    local = jnp.where(slab_rows_of(own_ref.shape) == slab_ref[0], local, 0.0)
    known = own_ref[...] + t1_ref[...] + t2_ref[...] + t3_ref[...]
    known = jnp.where(section == 0, local, known)
    up_ref[5 * cells :, :] = known
    down_ref[5 * cells :, :] = known
    for j, n in enumerate(EDGES):
        side, c_x = j // 5, VELOCITY[n][0]
        s_ref[8:own, :] = rl[j * REACH : (j + 1) * REACH, :]
        s_ref[own : own + cells, :] = e_ref[j]
        s_ref[own + cells : own + cells + REACH, :] = rr[j * REACH : (j + 1) * REACH, :]
        if c_x == 1:
            s_ref[7:8, :] = rl[EXTRA + side : EXTRA + side + 1, :]
        if c_x == -1:
            s_ref[own + cells + REACH : own + cells + REACH + 1, :] = rr[
                EXTRA + side : EXTRA + side + 1, :
            ]
        if side == 0:
            start, out = own - c_x + r, up_ref
            low, high = 1.0 - a, a
        else:
            start, out = own - c_x - r - 1, down_ref
            low, high = a, 1.0 - a
        line = s_ref[...]
        count = line.shape[0]
        line = low * line + high * pltpu.roll(line, count - 1, axis=0)
        at = (j % 5) * cells
        out[at : at + cells, :] = pltpu.roll(line, count - start, axis=0)[:cells]


VMEM = pl.BlockSpec(memory_space=pltpu.VMEM)
SMEM = pl.BlockSpec(memory_space=pltpu.SMEM)
HBM = pl.BlockSpec(memory_space=pltpu.HBM)
PARAMS = pltpu.CompilerParams(vmem_limit_bytes=24 * 1024 * 1024)


def near(*shape):
    return pltpu.VMEM(shape, jnp.float32)


def kept(*values):
    return tuple(pltpu.with_memory_space_constraint(v, pltpu.VMEM) for v in values)


def local(populations, offsets, fraction):
    _, slab_rows, cells, depth = shape = populations.shape
    slabs, flows = lax.axis_size("slab"), lax.axis_size("flow")
    all_cells = slab_rows * cells * depth * slabs * flows
    side = (5 * cells + 8, depth)
    table = (8, depth)
    both = ("slab", "flow")
    everyone = [(s, f) for s in range(slabs) for f in range(flows)]

    def beside(value, distance):
        route = [((i - distance) % flows, i) for i in range(flows)]
        return lax.ppermute(value, "flow", route)

    def displaced(value, slab_step, flow_step):
        route = [
            (((s + slab_step) % slabs) * flows + (f + flow_step) % flows, s * flows + f)
            for s, f in everyone
        ]
        return lax.ppermute(value, both, route)

    state = pltpu.HBM(shape, jnp.float32)
    edge_outs = (
        near(10, cells, depth),
        near(ROWS, depth),
        near(ROWS, depth),
    )
    buffers = [pltpu.VMEM(shape, jnp.float32)] * 2
    row_sems = [pltpu.SemaphoreType.DMA((slab_rows,))] * 2

    first = pl.pallas_call(
        first_kernel,
        out_shape=(state,) + edge_outs + (near(flows, 1, 128),) + (near(*table),) * 4,
        in_specs=[HBM],
        out_specs=(HBM,) + (VMEM,) * 8,
        scratch_shapes=buffers + [pltpu.VMEM((6, 8, depth), jnp.float32)] + row_sems,
        compiler_params=PARAMS,
        name="first",
    )
    walls = pl.pallas_call(
        wall_kernel,
        out_shape=(near(*side), near(*side)),
        in_specs=[SMEM] * 4 + [VMEM] * 8,
        out_specs=(VMEM,) * 2,
        scratch_shapes=[pltpu.VMEM((cells + 2 * REACH + 16, depth), jnp.float32)],
        compiler_params=PARAMS,
        name="walls",
    )
    following = pl.pallas_call(
        lambda *refs: next_kernel(all_cells, *refs),
        out_shape=(state,) + edge_outs + (near(*table), near(STEPS, 4)),
        in_specs=[SMEM, SMEM, HBM] + [VMEM] * 5,
        out_specs=(HBM,) + (VMEM,) * 5,
        scratch_shapes=buffers + row_sems,
        input_output_aliases={2: 0},
        compiler_params=PARAMS,
        name="following",
    )

    def leaf(blocks_apart):
        return lambda up, down: (
            displaced(up, -1, blocks_apart),
            displaced(down, 1, -blocks_apart),
        )

    def twig(start, count):
        leaves = [leaf(start + k) for k in range(count)]
        return lambda inner, up, down: lax.switch(inner, leaves, up, down)

    count = 4
    branches = [twig(start, count) for start in range(0, flows, count)]
    blocks = [((offsets[k] + REACH) // cells) % flows for k in range(STEPS)]

    slab = lax.axis_index("slab").reshape(1)

    def neighbours(mr, ml):
        return beside(mr, 1), beside(ml, -1)

    def apart(value, distance):
        return lax.ppermute(value, "slab", [(i, (i + distance) % slabs) for i in range(slabs)])

    def step(section, carry):
        p, edges, from_left, from_right, tables, _, now, *later = carry
        at = section.reshape(1)
        up, down = walls(
            at,
            slab,
            offsets,
            fraction,
            *kept(gathered, *tables, edges, from_left, from_right),
        )
        wu, wd = lax.switch(now // count, branches, now % count, up, down)
        p, edges, mr, ml, known, totals = following(
            at,
            slab,
            pltpu.with_memory_space_constraint(p, pltpu.HBM),
            *kept(from_left, from_right, wu, wd, up),
        )
        from_left, from_right, tables = lax.cond(
            section < STEPS - 1,
            lambda mr, ml, known, _: (
                *neighbours(mr, ml),
                (known, *(apart(known, k * STRIDE) for k in range(1, slabs // STRIDE))),
            ),
            lambda mr, ml, known, tables: (mr, ml, tables),
            mr,
            ml,
            known,
            tables,
        )
        return p, edges, from_left, from_right, tables, totals, *later, now

    p, edges, mr, ml, sums, *tables = first(pltpu.with_memory_space_constraint(populations, pltpu.HBM))
    from_left, from_right = neighbours(mr, ml)
    gathered = lax.all_to_all(sums, "flow", 0, 0)
    totals = jnp.zeros((STEPS, 4), jnp.float32)
    carry = (p, edges, from_left, from_right, tuple(tables), totals, *blocks)
    carry = lax.fori_loop(0, STEPS, step, carry)
    return carry[0], carry[5]


def solution(mesh):
    in_specs = (P(None, "slab", "flow", None), P(), P())
    out_specs = (P(None, "slab", "flow", None), P())
    return jax.shard_map(local, mesh=mesh, in_specs=in_specs, out_specs=out_specs, check_vma=False)
```

```python
import jax
import jax.numpy as jnp
from jax import lax
from jax.experimental import pallas as pl
from jax.experimental.pallas import tpu as pltpu
from jax.sharding import PartitionSpec as P

STEPS = 2
DEN = 64

VELOCITY = (
    (0, 0, 0),
    (1, 0, 0),
    (-1, 0, 0),
    (0, 1, 0),
    (0, -1, 0),
    (0, 0, 1),
    (0, 0, -1),
    (1, 1, 0),
    (-1, -1, 0),
    (1, -1, 0),
    (-1, 1, 0),
    (1, 0, 1),
    (-1, 0, -1),
    (1, 0, -1),
    (-1, 0, 1),
    (0, 1, 1),
    (0, -1, -1),
    (0, 1, -1),
    (0, -1, 1),
)
WEIGHTS = (1.0 / 3.0,) + (1.0 / 18.0,) * 6 + (1.0 / 36.0,) * 12
OMEGA = 1.0 / 1.4
SLIDE = 0.1
LEVEL = (0, 1, 2, 5, 6, 11, 12, 13, 14)
UPWARD = (3, 7, 10, 15, 17)
DOWNWARD = (4, 8, 9, 16, 18)
RIGHTWARD = (1, 7, 9, 11, 13)
LEFTWARD = (2, 8, 10, 12, 14)
EDGES = UPWARD + DOWNWARD
REACH = 16
HALO = 10 * REACH
EXTRA = HALO + 40
ROWS = EXTRA + 8
STRIDE = 4


def moments(f):
    diff = [None] + [f[2 * k - 1] - f[2 * k] for k in range(1, 10)]
    rho = f[0]
    for k in range(1, 10):
        rho = rho + (f[2 * k - 1] + f[2 * k])
    m_x = (diff[1] + diff[4]) + (diff[5] + diff[6]) + diff[7]
    m_y = (diff[2] + diff[4]) - (diff[5] - diff[8]) + diff[9]
    m_z = (diff[3] + diff[6]) - (diff[7] - diff[8]) - diff[9]
    return rho, m_x, m_y, m_z


def along(n, u_x, u_y, u_z):
    total = None
    for c, u in zip(VELOCITY[n], (u_x, u_y, u_z)):
        if c:
            term = u if c > 0 else -u
            total = term if total is None else total + term
    return total


def collide(f, rho, m_x, m_y, m_z):
    inverse = 1.0 / rho
    u_x, u_y, u_z = m_x * inverse, m_y * inverse, m_z * inverse
    base = 1.0 - 1.5 * (u_x * u_x + u_y * u_y + u_z * u_z)
    post = [(1.0 - OMEGA) * f[0] + (WEIGHTS[0] * OMEGA) * rho * base]
    for n in range(1, 19, 2):
        scale = (WEIGHTS[n] * OMEGA) * rho
        c_u = along(n, u_x, u_y, u_z)
        even = scale * (base + 4.5 * (c_u * c_u))
        odd = (3.0 * scale) * c_u
        post.append((1.0 - OMEGA) * f[n] + (even + odd))
        post.append((1.0 - OMEGA) * f[n + 1] + (even - odd))
    return post, u_x, u_y, u_z


def wall_change(n, rho, u_x, u_y, u_z, slide):
    c_x = VELOCITY[n][0]
    terms = -3.0 * slide * u_x - 1.5 * slide * slide
    if c_x:
        terms = terms + (
            3.0 * slide * c_x + 4.5 * slide * slide + (9.0 * slide * c_x) * along(n, u_x, u_y, u_z)
        )
    return (WEIGHTS[n] * rho) * terms


def roll_lanes(v, shift):
    return pltpu.roll(v, shift % v.shape[1], axis=1) if shift else v


def sum_of(values):
    total = values[0]
    for value in values[1:]:
        total = total + value
    return total


def store_edges(load, p_ref, y, side, e_ref, mr_ref, ml_ref, acc_ref):
    members, slide = ((UPWARD, -SLIDE), (DOWNWARD, SLIDE))[side]
    cells = e_ref.shape[1]
    for lo in range(0, cells, 8):
        rows = slice(lo, lo + 8)
        rho, m_x, m_y, m_z = moments(load(y, lo))
        inverse = 1.0 / rho
        u_x, u_y, u_z = m_x * inverse, m_y * inverse, m_z * inverse
        values = []
        for k, n in enumerate(members):
            j = 5 * side + k
            value = p_ref[n, y, rows, :] + wall_change(n, rho, u_x, u_y, u_z, slide)
            values.append(value)
            e_ref[j, rows, :] = value
            if lo < REACH:
                ml_ref[j * REACH + lo : j * REACH + lo + 8, :] = value
            if lo >= cells - REACH:
                at = j * REACH + lo - (cells - REACH)
                mr_ref[at : at + 8, :] = value
            if VELOCITY[n][0] == 1 and lo == cells - REACH - 8:
                mr_ref[EXTRA + side : EXTRA + side + 1, :] = value[7:8]
            if VELOCITY[n][0] == -1 and lo == REACH:
                ml_ref[EXTRA + side : EXTRA + side + 1, :] = value[0:1]
        if acc_ref is not None:
            acc_ref[5] += (slide / 3.0) * sum_of(values)


def collide_row(y, load, p_ref, mr_ref, ml_ref, acc_ref, slab_rows):
    cells = p_ref.shape[2]
    for lo in range(0, cells, 8):
        rows = slice(lo, lo + 8)
        f = load(y, lo)
        rho, m_x, m_y, m_z = moments(f)
        post = collide(f, rho, m_x, m_y, m_z)[0]
        for n in range(19):
            p_ref[n, y, rows, :] = post[n]
        if acc_ref is not None:
            acc_ref[0] += rho
            acc_ref[1] += m_x
            acc_ref[2] += m_y
            acc_ref[3] += m_z
            top, bottom = y == slab_rows - 1, y == 0
            edge = jnp.where(bottom, SLIDE, 0.0) - jnp.where(top, SLIDE, 0.0)
            both = jnp.where(bottom | top, SLIDE, 0.0)
            acc_ref[4] += (edge / 6.0) * rho - (both / 2.0) * m_y
            level, up, down = (sum_of([post[n] for n in ns]) for ns in (LEVEL, UPWARD, DOWNWARD))
            below_top = jnp.where(y == slab_rows - 2, -SLIDE * 2.0 / 3.0, 0.0)
            above_bottom = jnp.where(y == 1, SLIDE * 2.0 / 3.0, 0.0)
            acc_ref[5] += (edge / 6.0) * level + (below_top * up + above_bottom * down)
    for k, n in enumerate(RIGHTWARD):
        mr_ref[pl.ds(HALO + 8 * k + y, 1), :] = p_ref[n, y, cells - 1 : cells, :]
    for k, n in enumerate(LEFTWARD):
        ml_ref[pl.ds(HALO + 8 * k + y, 1), :] = p_ref[n, y, 0:1, :]


def clear_rest(*messages):
    for message in messages:
        message[EXTRA:ROWS, :] = jnp.zeros((ROWS - EXTRA, message.shape[1]), jnp.float32)


def first_kernel(
    f_hbm,
    p_hbm,
    e_ref,
    mr_ref,
    ml_ref,
    t_ref,
    t0_ref,
    t1_ref,
    t2_ref,
    t3_ref,
    f_ref,
    p_ref,
    acc_ref,
    in_sems,
    out_sems,
):
    slab_rows = f_ref.shape[1]

    def arriving(y):
        return pltpu.make_async_copy(f_hbm.at[:, y], f_ref.at[:, y], in_sems.at[y])

    def leaving(y):
        return pltpu.make_async_copy(p_ref.at[:, y], p_hbm.at[:, y], out_sems.at[y])

    for y in range(slab_rows):
        arriving(y).start()
    acc_ref[...] = jnp.zeros_like(acc_ref)
    clear_rest(mr_ref, ml_ref)
    for table in (t0_ref, t1_ref, t2_ref, t3_ref):
        table[...] = jnp.zeros_like(table)

    def load(y, lo):
        return [f_ref[n, y, lo : lo + 8, :] for n in range(19)]

    def step(y, carry):
        arriving(y).wait()
        collide_row(y, load, p_ref, mr_ref, ml_ref, acc_ref, slab_rows)
        leaving(y).start()
        return carry

    lax.fori_loop(0, slab_rows, step, 0)
    store_edges(load, p_ref, slab_rows - 1, 0, e_ref, mr_ref, ml_ref, acc_ref)
    store_edges(load, p_ref, 0, 1, e_ref, mr_ref, ml_ref, acc_ref)
    lane = lax.broadcasted_iota(jnp.int32, t_ref.shape, 2)
    out = jnp.zeros(t_ref.shape, jnp.float32)
    for q in range(6):
        out = out + jnp.where(lane == q, jnp.sum(acc_ref[q]), 0.0)
    t_ref[...] = out
    for y in range(slab_rows):
        leaving(y).wait()


def streamed(p_ref, rl, rr, wu, wd, slab_rows):
    cells = p_ref.shape[2]
    row = lax.broadcasted_iota(jnp.int32, (8, p_ref.shape[3]), 0)

    def load(y, lo):
        out = []
        for n, (c_x, c_y, c_z) in enumerate(VELOCITY):
            if c_y == 1 and isinstance(y, int) and y == 0:
                v = wu[UPWARD.index(n) * cells + lo : UPWARD.index(n) * cells + lo + 8, :]
            elif c_y == -1 and isinstance(y, int) and y == slab_rows - 1:
                v = wd[DOWNWARD.index(n) * cells + lo : DOWNWARD.index(n) * cells + lo + 8, :]
            elif c_x == 1 and lo == 0:
                halo = rl[pl.ds(HALO + 8 * RIGHTWARD.index(n) + y - c_y, 1), :]
                v = jnp.where(row == 0, halo, pltpu.roll(p_ref[n, y - c_y, 0:8, :], 1, axis=0))
            elif c_x == -1 and lo == cells - 8:
                halo = rr[pl.ds(HALO + 8 * LEFTWARD.index(n) + y - c_y, 1), :]
                v = jnp.where(
                    row == 7, halo, pltpu.roll(p_ref[n, y - c_y, cells - 8 : cells, :], 7, axis=0)
                )
            else:
                v = p_ref[n, y - c_y, lo - c_x : lo - c_x + 8, :]
            out.append(roll_lanes(v, c_z))
        return out

    return load


def next_kernel(
    all_cells,
    step_ref,
    slab_ref,
    p_hbm,
    rl,
    rr,
    wu,
    wd,
    up_ref,
    o_hbm,
    e_ref,
    mr_ref,
    ml_ref,
    t_ref,
    s_hbm,
    p_ref,
    q_ref,
    s_ref,
    in_sems,
    out_sems,
    s_sem,
):
    slab_rows, cells = p_ref.shape[1:3]

    def arriving(y):
        return pltpu.make_async_copy(p_hbm.at[:, y], p_ref.at[:, y], in_sems.at[y])

    def leaving(y):
        return pltpu.make_async_copy(q_ref.at[:, y], o_hbm.at[:, y], out_sems.at[y])

    for y in range(slab_rows):
        arriving(y).start()
    clear_rest(mr_ref, ml_ref)
    known, below, above = (ref[5 * cells :, :] for ref in (up_ref, wu, wd))
    t_ref[...] = known + below + above
    ahead = (slab_rows_of(known.shape) - slab_ref[0]) & (STRIDE - 1)
    total = jnp.sum(jnp.where(ahead == 2, above, known), axis=0, keepdims=True)
    total = (total[:, :128] + total[:, 128:]) * (1.0 / all_cells)
    lane = lax.broadcasted_iota(jnp.int32, total.shape, 1)
    rho, m_x, m_y, m_z, first, second = (
        jnp.sum(jnp.where(lane == q, total, 0.0)) for q in range(6)
    )
    at = lax.broadcasted_iota(jnp.int32, s_ref.shape, 1)
    x = m_x + first + jnp.where(lax.broadcasted_iota(jnp.int32, s_ref.shape, 0) == 1, second, 0.0)
    s_ref[...] = jnp.where(at == 0, rho, jnp.where(at == 1, x, jnp.where(at == 2, m_y, m_z)))
    totals = pltpu.make_async_copy(s_ref, s_hbm, s_sem)
    totals.start()

    load = streamed(p_ref, rl, rr, wu, wd, slab_rows)

    def all_rows(work):
        def step(y, carry):
            arriving(y + 1).wait()
            work(y)
            leaving(y).start()
            return carry

        arriving(0).wait()
        step(0, 0)
        lax.fori_loop(1, slab_rows - 1, step, 0)
        work(slab_rows - 1)
        leaving(slab_rows - 1).start()

    def store(y):
        for lo in range(0, cells, 8):
            for n, v in enumerate(load(y, lo)):
                q_ref[n, y, lo : lo + 8, :] = v

    @pl.when(step_ref[0] < STEPS - 1)
    def _():
        all_rows(lambda y: collide_row(y, load, q_ref, mr_ref, ml_ref, None, slab_rows))
        store_edges(load, q_ref, slab_rows - 1, 0, e_ref, mr_ref, ml_ref, None)
        store_edges(load, q_ref, 0, 1, e_ref, mr_ref, ml_ref, None)

    @pl.when(step_ref[0] == STEPS - 1)
    def _():
        all_rows(store)

    totals.wait()
    for y in range(slab_rows):
        leaving(y).wait()


def slab_rows_of(shape):
    half = jnp.where(lax.broadcasted_iota(jnp.int32, shape, 1) >= shape[1] // 2, 1, 0)
    return lax.broadcasted_iota(jnp.int32, shape, 0) + shape[0] * half


def wall_kernel(
    step_ref,
    slab_ref,
    d_ref,
    n_ref,
    g_ref,
    own_ref,
    t1_ref,
    t2_ref,
    t3_ref,
    e_ref,
    rl,
    rr,
    up_ref,
    down_ref,
    s_ref,
):
    cells = e_ref.shape[1]
    own = REACH + 8
    section = step_ref[0]
    r = lax.rem(d_ref[section] + REACH, cells) - REACH
    a = n_ref[section].astype(jnp.float32) * (1.0 / DEN)
    local = jnp.sum(g_ref[...], axis=0)
    local = jnp.broadcast_to(jnp.concatenate([local, local], axis=1), own_ref.shape)
    local = jnp.where(slab_rows_of(own_ref.shape) == slab_ref[0], local, 0.0)
    known = own_ref[...] + t1_ref[...] + t2_ref[...] + t3_ref[...]
    known = jnp.where(section == 0, local, known)
    up_ref[5 * cells :, :] = known
    down_ref[5 * cells :, :] = known
    for j, n in enumerate(EDGES):
        side, c_x = j // 5, VELOCITY[n][0]
        s_ref[8:own, :] = rl[j * REACH : (j + 1) * REACH, :]
        s_ref[own : own + cells, :] = e_ref[j]
        s_ref[own + cells : own + cells + REACH, :] = rr[j * REACH : (j + 1) * REACH, :]
        if c_x == 1:
            s_ref[7:8, :] = rl[EXTRA + side : EXTRA + side + 1, :]
        if c_x == -1:
            s_ref[own + cells + REACH : own + cells + REACH + 1, :] = rr[
                EXTRA + side : EXTRA + side + 1, :
            ]
        if side == 0:
            start, out = own - c_x + r, up_ref
            low, high = 1.0 - a, a
        else:
            start, out = own - c_x - r - 1, down_ref
            low, high = a, 1.0 - a
        line = s_ref[...]
        count = line.shape[0]
        line = low * line + high * pltpu.roll(line, count - 1, axis=0)
        at = (j % 5) * cells
        out[at : at + cells, :] = pltpu.roll(line, count - start, axis=0)[:cells]


VMEM = pl.BlockSpec(memory_space=pltpu.VMEM)
SMEM = pl.BlockSpec(memory_space=pltpu.SMEM)
HBM = pl.BlockSpec(memory_space=pltpu.HBM)
PARAMS = pltpu.CompilerParams(vmem_limit_bytes=24 * 1024 * 1024)


def near(*shape):
    return pltpu.VMEM(shape, jnp.float32)


def kept(*values):
    return tuple(pltpu.with_memory_space_constraint(v, pltpu.VMEM) for v in values)


def local(populations, offsets, fraction):
    _, slab_rows, cells, depth = shape = populations.shape
    slabs, flows = lax.axis_size("slab"), lax.axis_size("flow")
    all_cells = slab_rows * cells * depth * slabs * flows
    side = (5 * cells + 8, depth)
    table = (8, depth)
    both = ("slab", "flow")
    everyone = [(s, f) for s in range(slabs) for f in range(flows)]

    def beside(value, distance):
        route = [((i - distance) % flows, i) for i in range(flows)]
        return lax.ppermute(value, "flow", route)

    def displaced(value, slab_step, flow_step):
        route = [
            (((s + slab_step) % slabs) * flows + (f + flow_step) % flows, s * flows + f)
            for s, f in everyone
        ]
        return lax.ppermute(value, both, route)

    state = pltpu.HBM(shape, jnp.float32)
    edge_outs = (
        near(10, cells, depth),
        near(ROWS, depth),
        near(ROWS, depth),
    )
    buffers = [pltpu.VMEM(shape, jnp.float32)] * 2
    row_sems = [pltpu.SemaphoreType.DMA((slab_rows,))] * 2

    first = pl.pallas_call(
        first_kernel,
        out_shape=(state,) + edge_outs + (near(flows, 1, 128),) + (near(*table),) * 4,
        in_specs=[HBM],
        out_specs=(HBM,) + (VMEM,) * 8,
        scratch_shapes=buffers + [pltpu.VMEM((6, 8, depth), jnp.float32)] + row_sems,
        compiler_params=PARAMS,
        name="first",
    )
    walls = pl.pallas_call(
        wall_kernel,
        out_shape=(near(*side), near(*side)),
        in_specs=[SMEM] * 4 + [VMEM] * 8,
        out_specs=(VMEM,) * 2,
        scratch_shapes=[pltpu.VMEM((cells + 2 * REACH + 16, depth), jnp.float32)],
        compiler_params=PARAMS,
        name="walls",
    )
    following = pl.pallas_call(
        lambda *refs: next_kernel(all_cells, *refs),
        out_shape=(state,) + edge_outs + (near(*table), pltpu.HBM((STEPS, 4), jnp.float32)),
        in_specs=[SMEM, SMEM, HBM] + [VMEM] * 5,
        out_specs=(HBM,) + (VMEM,) * 4 + (HBM,),
        scratch_shapes=buffers
        + [pltpu.VMEM((STEPS, 4), jnp.float32)]
        + row_sems
        + [pltpu.SemaphoreType.DMA],
        input_output_aliases={2: 0},
        compiler_params=PARAMS,
        name="following",
    )

    def leaf(blocks_apart):
        return lambda up, down: (
            displaced(up, -1, blocks_apart),
            displaced(down, 1, -blocks_apart),
        )

    def twig(start, count):
        leaves = [leaf(start + k) for k in range(count)]
        return lambda inner, up, down: lax.switch(inner, leaves, up, down)

    count = 4
    branches = [twig(start, count) for start in range(0, flows, count)]
    blocks = [((offsets[k] + REACH) // cells) % flows for k in range(STEPS)]

    slab = lax.axis_index("slab").reshape(1)

    def neighbours(mr, ml):
        return beside(mr, 1), beside(ml, -1)

    def apart(value, distance):
        return lax.ppermute(value, "slab", [(i, (i + distance) % slabs) for i in range(slabs)])

    def step(section, carry):
        p, edges, from_left, from_right, tables, _, now, *later = carry
        at = section.reshape(1)
        up, down = walls(
            at,
            slab,
            offsets,
            fraction,
            *kept(gathered, *tables, edges, from_left, from_right),
        )
        wu, wd = lax.switch(now // count, branches, now % count, up, down)
        p, edges, mr, ml, known, totals = following(
            at,
            slab,
            pltpu.with_memory_space_constraint(p, pltpu.HBM),
            *kept(from_left, from_right, wu, wd, up),
        )
        from_left, from_right, tables = lax.cond(
            section < STEPS - 1,
            lambda mr, ml, known, _: (
                *neighbours(mr, ml),
                (known, *(apart(known, k * STRIDE) for k in range(1, slabs // STRIDE))),
            ),
            lambda mr, ml, known, tables: (mr, ml, tables),
            mr,
            ml,
            known,
            tables,
        )
        return p, edges, from_left, from_right, tables, totals, *later, now

    p, edges, mr, ml, sums, *tables = first(pltpu.with_memory_space_constraint(populations, pltpu.HBM))
    from_left, from_right = neighbours(mr, ml)
    gathered = lax.all_to_all(sums, "flow", 0, 0)
    totals = jnp.zeros((STEPS, 4), jnp.float32)
    carry = (p, edges, from_left, from_right, tuple(tables), totals, *blocks)
    carry = lax.fori_loop(0, STEPS, step, carry)
    return carry[0], carry[5]


def solution(mesh):
    in_specs = (P(None, "slab", "flow", None), P(), P())
    out_specs = (P(None, "slab", "flow", None), P())
    return jax.shard_map(local, mesh=mesh, in_specs=in_specs, out_specs=out_specs, check_vma=False)
```

```python
import jax
import jax.numpy as jnp
from jax import lax
from jax.experimental import pallas as pl
from jax.experimental.pallas import tpu as pltpu
from jax.sharding import PartitionSpec as P

STEPS = 2
DEN = 64

VELOCITY = (
    (0, 0, 0),
    (1, 0, 0),
    (-1, 0, 0),
    (0, 1, 0),
    (0, -1, 0),
    (0, 0, 1),
    (0, 0, -1),
    (1, 1, 0),
    (-1, -1, 0),
    (1, -1, 0),
    (-1, 1, 0),
    (1, 0, 1),
    (-1, 0, -1),
    (1, 0, -1),
    (-1, 0, 1),
    (0, 1, 1),
    (0, -1, -1),
    (0, 1, -1),
    (0, -1, 1),
)
WEIGHTS = (1.0 / 3.0,) + (1.0 / 18.0,) * 6 + (1.0 / 36.0,) * 12
OMEGA = 1.0 / 1.4
SLIDE = 0.1
LEVEL = (0, 1, 2, 5, 6, 11, 12, 13, 14)
UPWARD = (3, 7, 10, 15, 17)
DOWNWARD = (4, 8, 9, 16, 18)
RIGHTWARD = (1, 7, 9, 11, 13)
LEFTWARD = (2, 8, 10, 12, 14)
EDGES = UPWARD + DOWNWARD
REACH = 16
HALO = 10 * REACH
EXTRA = HALO + 40
ROWS = EXTRA + 8
STRIDE = 4


def moments(f):
    diff = [None] + [f[2 * k - 1] - f[2 * k] for k in range(1, 10)]
    rho = f[0]
    for k in range(1, 10):
        rho = rho + (f[2 * k - 1] + f[2 * k])
    m_x = (diff[1] + diff[4]) + (diff[5] + diff[6]) + diff[7]
    m_y = (diff[2] + diff[4]) - (diff[5] - diff[8]) + diff[9]
    m_z = (diff[3] + diff[6]) - (diff[7] - diff[8]) - diff[9]
    return rho, m_x, m_y, m_z


def along(n, u_x, u_y, u_z):
    total = None
    for c, u in zip(VELOCITY[n], (u_x, u_y, u_z)):
        if c:
            term = u if c > 0 else -u
            total = term if total is None else total + term
    return total


def collide(f, rho, m_x, m_y, m_z):
    inverse = 1.0 / rho
    u_x, u_y, u_z = m_x * inverse, m_y * inverse, m_z * inverse
    base = 1.0 - 1.5 * (u_x * u_x + u_y * u_y + u_z * u_z)
    post = [(1.0 - OMEGA) * f[0] + (WEIGHTS[0] * OMEGA) * rho * base]
    for n in range(1, 19, 2):
        scale = (WEIGHTS[n] * OMEGA) * rho
        c_u = along(n, u_x, u_y, u_z)
        even = scale * (base + 4.5 * (c_u * c_u))
        odd = (3.0 * scale) * c_u
        post.append((1.0 - OMEGA) * f[n] + (even + odd))
        post.append((1.0 - OMEGA) * f[n + 1] + (even - odd))
    return post, u_x, u_y, u_z


def wall_change(n, rho, u_x, u_y, u_z, slide):
    c_x = VELOCITY[n][0]
    terms = -3.0 * slide * u_x - 1.5 * slide * slide
    if c_x:
        terms = terms + (
            3.0 * slide * c_x + 4.5 * slide * slide + (9.0 * slide * c_x) * along(n, u_x, u_y, u_z)
        )
    return (WEIGHTS[n] * rho) * terms


def roll_lanes(v, shift):
    return pltpu.roll(v, shift % v.shape[1], axis=1) if shift else v


def sum_of(values):
    total = values[0]
    for value in values[1:]:
        total = total + value
    return total


def store_edges(load, p_ref, y, side, e_ref, mr_ref, ml_ref, acc_ref):
    members, slide = ((UPWARD, -SLIDE), (DOWNWARD, SLIDE))[side]
    cells = e_ref.shape[1]
    for lo in range(0, cells, 8):
        rows = slice(lo, lo + 8)
        rho, m_x, m_y, m_z = moments(load(y, lo))
        inverse = 1.0 / rho
        u_x, u_y, u_z = m_x * inverse, m_y * inverse, m_z * inverse
        values = []
        for k, n in enumerate(members):
            j = 5 * side + k
            value = p_ref[n, y, rows, :] + wall_change(n, rho, u_x, u_y, u_z, slide)
            values.append(value)
            e_ref[j, rows, :] = value
            if lo < REACH:
                ml_ref[j * REACH + lo : j * REACH + lo + 8, :] = value
            if lo >= cells - REACH:
                at = j * REACH + lo - (cells - REACH)
                mr_ref[at : at + 8, :] = value
            if VELOCITY[n][0] == 1 and lo == cells - REACH - 8:
                mr_ref[EXTRA + side : EXTRA + side + 1, :] = value[7:8]
            if VELOCITY[n][0] == -1 and lo == REACH:
                ml_ref[EXTRA + side : EXTRA + side + 1, :] = value[0:1]
        if acc_ref is not None:
            acc_ref[5] += (slide / 3.0) * sum_of(values)


def collide_row(y, load, p_ref, mr_ref, ml_ref, acc_ref, slab_rows):
    cells = p_ref.shape[2]
    for lo in range(0, cells, 8):
        rows = slice(lo, lo + 8)
        f = load(y, lo)
        rho, m_x, m_y, m_z = moments(f)
        post = collide(f, rho, m_x, m_y, m_z)[0]
        for n in range(19):
            p_ref[n, y, rows, :] = post[n]
        if acc_ref is not None:
            acc_ref[0] += rho
            acc_ref[1] += m_x
            acc_ref[2] += m_y
            acc_ref[3] += m_z
            top, bottom = y == slab_rows - 1, y == 0
            edge = jnp.where(bottom, SLIDE, 0.0) - jnp.where(top, SLIDE, 0.0)
            both = jnp.where(bottom | top, SLIDE, 0.0)
            acc_ref[4] += (edge / 6.0) * rho - (both / 2.0) * m_y
            level, up, down = (sum_of([post[n] for n in ns]) for ns in (LEVEL, UPWARD, DOWNWARD))
            below_top = jnp.where(y == slab_rows - 2, -SLIDE * 2.0 / 3.0, 0.0)
            above_bottom = jnp.where(y == 1, SLIDE * 2.0 / 3.0, 0.0)
            acc_ref[5] += (edge / 6.0) * level + (below_top * up + above_bottom * down)
    for k, n in enumerate(RIGHTWARD):
        mr_ref[pl.ds(HALO + 8 * k + y, 1), :] = p_ref[n, y, cells - 1 : cells, :]
    for k, n in enumerate(LEFTWARD):
        ml_ref[pl.ds(HALO + 8 * k + y, 1), :] = p_ref[n, y, 0:1, :]


def clear_rest(*messages):
    for message in messages:
        message[EXTRA:ROWS, :] = jnp.zeros((ROWS - EXTRA, message.shape[1]), jnp.float32)


def first_kernel(
    f_hbm,
    p_hbm,
    e_ref,
    mr_ref,
    ml_ref,
    t_ref,
    t0_ref,
    t1_ref,
    t2_ref,
    t3_ref,
    f_ref,
    p_ref,
    acc_ref,
    in_sems,
    out_sems,
):
    slab_rows = f_ref.shape[1]

    def arriving(y):
        return pltpu.make_async_copy(f_hbm.at[:, y], f_ref.at[:, y], in_sems.at[y])

    def leaving(y):
        return pltpu.make_async_copy(p_ref.at[:, y], p_hbm.at[:, y], out_sems.at[y])

    for y in range(slab_rows):
        arriving(y).start()
    acc_ref[...] = jnp.zeros_like(acc_ref)
    clear_rest(mr_ref, ml_ref)
    for table in (t0_ref, t1_ref, t2_ref, t3_ref):
        table[...] = jnp.zeros_like(table)

    def load(y, lo):
        return [f_ref[n, y, lo : lo + 8, :] for n in range(19)]

    def step(y, carry):
        arriving(y).wait()
        collide_row(y, load, p_ref, mr_ref, ml_ref, acc_ref, slab_rows)
        leaving(y).start()
        return carry

    lax.fori_loop(0, slab_rows, step, 0)
    store_edges(load, p_ref, slab_rows - 1, 0, e_ref, mr_ref, ml_ref, acc_ref)
    store_edges(load, p_ref, 0, 1, e_ref, mr_ref, ml_ref, acc_ref)
    lane = lax.broadcasted_iota(jnp.int32, t_ref.shape, 2)
    out = jnp.zeros(t_ref.shape, jnp.float32)
    for q in range(6):
        out = out + jnp.where(lane == q, jnp.sum(acc_ref[q]), 0.0)
    t_ref[...] = out
    for y in range(slab_rows):
        leaving(y).wait()


def streamed(p_ref, rl, rr, wu, wd, slab_rows):
    cells = p_ref.shape[2]
    row = lax.broadcasted_iota(jnp.int32, (8, p_ref.shape[3]), 0)

    def load(y, lo):
        out = []
        for n, (c_x, c_y, c_z) in enumerate(VELOCITY):
            if c_y == 1 and isinstance(y, int) and y == 0:
                v = wu[UPWARD.index(n) * cells + lo : UPWARD.index(n) * cells + lo + 8, :]
            elif c_y == -1 and isinstance(y, int) and y == slab_rows - 1:
                v = wd[DOWNWARD.index(n) * cells + lo : DOWNWARD.index(n) * cells + lo + 8, :]
            elif c_x == 1 and lo == 0:
                halo = rl[pl.ds(HALO + 8 * RIGHTWARD.index(n) + y - c_y, 1), :]
                v = jnp.where(row == 0, halo, pltpu.roll(p_ref[n, y - c_y, 0:8, :], 1, axis=0))
            elif c_x == -1 and lo == cells - 8:
                halo = rr[pl.ds(HALO + 8 * LEFTWARD.index(n) + y - c_y, 1), :]
                v = jnp.where(
                    row == 7, halo, pltpu.roll(p_ref[n, y - c_y, cells - 8 : cells, :], 7, axis=0)
                )
            else:
                v = p_ref[n, y - c_y, lo - c_x : lo - c_x + 8, :]
            out.append(roll_lanes(v, c_z))
        return out

    return load


def next_kernel(
    all_cells,
    step_ref,
    slab_ref,
    p_hbm,
    rl,
    rr,
    wu,
    wd,
    up_ref,
    o_hbm,
    e_ref,
    mr_ref,
    ml_ref,
    t_ref,
    s_hbm,
    p_ref,
    q_ref,
    s_ref,
    in_sems,
    out_sems,
    s_sem,
):
    slab_rows, cells = p_ref.shape[1:3]

    def arriving(y):
        return pltpu.make_async_copy(p_hbm.at[:, y], p_ref.at[:, y], in_sems.at[y])

    def leaving(y):
        return pltpu.make_async_copy(q_ref.at[:, y], o_hbm.at[:, y], out_sems.at[y])

    for y in range(slab_rows):
        arriving(y).start()
    clear_rest(mr_ref, ml_ref)
    known, below, above = (ref[5 * cells :, :] for ref in (up_ref, wu, wd))
    t_ref[...] = known + below + above
    ahead = (slab_rows_of(known.shape) - slab_ref[0]) & (STRIDE - 1)
    total = jnp.sum(jnp.where(ahead == 2, above, known), axis=0, keepdims=True)
    total = (total[:, :128] + total[:, 128:]) * (1.0 / all_cells)
    lane = lax.broadcasted_iota(jnp.int32, total.shape, 1)
    rho, m_x, m_y, m_z, first, second = (
        jnp.sum(jnp.where(lane == q, total, 0.0)) for q in range(6)
    )
    at = lax.broadcasted_iota(jnp.int32, s_ref.shape, 1)
    x = m_x + first + jnp.where(lax.broadcasted_iota(jnp.int32, s_ref.shape, 0) == 1, second, 0.0)
    s_ref[...] = jnp.where(at == 0, rho, jnp.where(at == 1, x, jnp.where(at == 2, m_y, m_z)))
    totals = pltpu.make_async_copy(s_ref, s_hbm, s_sem)
    totals.start()

    load = streamed(p_ref, rl, rr, wu, wd, slab_rows)

    def all_rows(work):
        def step(y, carry):
            arriving(y + 1).wait()
            work(y)
            leaving(y).start()
            return carry

        arriving(0).wait()
        step(0, 0)
        lax.fori_loop(1, slab_rows - 1, step, 0)
        work(slab_rows - 1)
        leaving(slab_rows - 1).start()

    def store(y):
        for lo in range(0, cells, 8):
            for n, v in enumerate(load(y, lo)):
                q_ref[n, y, lo : lo + 8, :] = v

    @pl.when(step_ref[0] < STEPS - 1)
    def _():
        all_rows(lambda y: collide_row(y, load, q_ref, mr_ref, ml_ref, None, slab_rows))
        store_edges(load, q_ref, slab_rows - 1, 0, e_ref, mr_ref, ml_ref, None)
        store_edges(load, q_ref, 0, 1, e_ref, mr_ref, ml_ref, None)

    @pl.when(step_ref[0] == STEPS - 1)
    def _():
        all_rows(store)

    totals.wait()
    for y in range(slab_rows):
        leaving(y).wait()


def slab_rows_of(shape):
    half = jnp.where(lax.broadcasted_iota(jnp.int32, shape, 1) >= shape[1] // 2, 1, 0)
    return lax.broadcasted_iota(jnp.int32, shape, 0) + shape[0] * half


def wall_kernel(
    step_ref,
    slab_ref,
    d_ref,
    n_ref,
    g_ref,
    own_ref,
    t1_ref,
    t2_ref,
    t3_ref,
    e_ref,
    rl,
    rr,
    up_ref,
    down_ref,
    s_ref,
):
    cells = e_ref.shape[1]
    own = REACH + 8
    section = step_ref[0]
    r = lax.rem(d_ref[section] + REACH, cells) - REACH
    a = n_ref[section].astype(jnp.float32) * (1.0 / DEN)
    local = jnp.sum(g_ref[...], axis=0)
    local = jnp.broadcast_to(jnp.concatenate([local, local], axis=1), own_ref.shape)
    local = jnp.where(slab_rows_of(own_ref.shape) == slab_ref[0], local, 0.0)
    known = own_ref[...] + t1_ref[...] + t2_ref[...] + t3_ref[...]
    known = jnp.where(section == 0, local, known)
    up_ref[5 * cells :, :] = known
    down_ref[5 * cells :, :] = known
    for j, n in enumerate(EDGES):
        side, c_x = j // 5, VELOCITY[n][0]
        s_ref[8:own, :] = rl[j * REACH : (j + 1) * REACH, :]
        s_ref[own : own + cells, :] = e_ref[j]
        s_ref[own + cells : own + cells + REACH, :] = rr[j * REACH : (j + 1) * REACH, :]
        if c_x == 1:
            s_ref[7:8, :] = rl[EXTRA + side : EXTRA + side + 1, :]
        if c_x == -1:
            s_ref[own + cells + REACH : own + cells + REACH + 1, :] = rr[
                EXTRA + side : EXTRA + side + 1, :
            ]
        if side == 0:
            start, out = own - c_x + r, up_ref
            low, high = 1.0 - a, a
        else:
            start, out = own - c_x - r - 1, down_ref
            low, high = a, 1.0 - a
        count = cells + 2 * REACH + 16
        line = low * s_ref[0:count, :] + high * s_ref[1 : count + 1, :]
        at = (j % 5) * cells
        out[at : at + cells, :] = pltpu.roll(line, count - start, axis=0)[:cells]


VMEM = pl.BlockSpec(memory_space=pltpu.VMEM)
SMEM = pl.BlockSpec(memory_space=pltpu.SMEM)
HBM = pl.BlockSpec(memory_space=pltpu.HBM)
PARAMS = pltpu.CompilerParams(vmem_limit_bytes=24 * 1024 * 1024)


def near(*shape):
    return pltpu.VMEM(shape, jnp.float32)


def kept(*values):
    return tuple(pltpu.with_memory_space_constraint(v, pltpu.VMEM) for v in values)


def local(populations, offsets, fraction):
    _, slab_rows, cells, depth = shape = populations.shape
    slabs, flows = lax.axis_size("slab"), lax.axis_size("flow")
    all_cells = slab_rows * cells * depth * slabs * flows
    side = (5 * cells + 8, depth)
    table = (8, depth)
    both = ("slab", "flow")
    everyone = [(s, f) for s in range(slabs) for f in range(flows)]

    def beside(value, distance):
        route = [((i - distance) % flows, i) for i in range(flows)]
        return lax.ppermute(value, "flow", route)

    def displaced(value, slab_step, flow_step):
        route = [
            (((s + slab_step) % slabs) * flows + (f + flow_step) % flows, s * flows + f)
            for s, f in everyone
        ]
        return lax.ppermute(value, both, route)

    state = pltpu.HBM(shape, jnp.float32)
    edge_outs = (
        near(10, cells, depth),
        near(ROWS, depth),
        near(ROWS, depth),
    )
    buffers = [pltpu.VMEM(shape, jnp.float32)] * 2
    row_sems = [pltpu.SemaphoreType.DMA((slab_rows,))] * 2

    first = pl.pallas_call(
        first_kernel,
        out_shape=(state,) + edge_outs + (near(flows, 1, 128),) + (near(*table),) * 4,
        in_specs=[HBM],
        out_specs=(HBM,) + (VMEM,) * 8,
        scratch_shapes=buffers + [pltpu.VMEM((6, 8, depth), jnp.float32)] + row_sems,
        compiler_params=PARAMS,
        name="first",
    )
    walls = pl.pallas_call(
        wall_kernel,
        out_shape=(near(*side), near(*side)),
        in_specs=[SMEM] * 4 + [VMEM] * 8,
        out_specs=(VMEM,) * 2,
        scratch_shapes=[pltpu.VMEM((cells + 2 * REACH + 24, depth), jnp.float32)],
        compiler_params=PARAMS,
        name="walls",
    )
    following = pl.pallas_call(
        lambda *refs: next_kernel(all_cells, *refs),
        out_shape=(state,) + edge_outs + (near(*table), pltpu.HBM((STEPS, 4), jnp.float32)),
        in_specs=[SMEM, SMEM, HBM] + [VMEM] * 5,
        out_specs=(HBM,) + (VMEM,) * 4 + (HBM,),
        scratch_shapes=buffers
        + [pltpu.VMEM((STEPS, 4), jnp.float32)]
        + row_sems
        + [pltpu.SemaphoreType.DMA],
        input_output_aliases={2: 0},
        compiler_params=PARAMS,
        name="following",
    )

    def leaf(blocks_apart):
        return lambda up, down: (
            displaced(up, -1, blocks_apart),
            displaced(down, 1, -blocks_apart),
        )

    def twig(start, count):
        leaves = [leaf(start + k) for k in range(count)]
        return lambda inner, up, down: lax.switch(inner, leaves, up, down)

    count = 4
    branches = [twig(start, count) for start in range(0, flows, count)]
    blocks = [((offsets[k] + REACH) // cells) % flows for k in range(STEPS)]

    slab = lax.axis_index("slab").reshape(1)

    def neighbours(mr, ml):
        return beside(mr, 1), beside(ml, -1)

    def apart(value, distance):
        return lax.ppermute(value, "slab", [(i, (i + distance) % slabs) for i in range(slabs)])

    def step(section, carry):
        p, edges, from_left, from_right, tables, _, now, *later = carry
        at = section.reshape(1)
        up, down = walls(
            at,
            slab,
            offsets,
            fraction,
            *kept(gathered, *tables, edges, from_left, from_right),
        )
        wu, wd = lax.switch(now // count, branches, now % count, up, down)
        p, edges, mr, ml, known, totals = following(
            at,
            slab,
            pltpu.with_memory_space_constraint(p, pltpu.HBM),
            *kept(from_left, from_right, wu, wd, up),
        )
        from_left, from_right, tables = lax.cond(
            section < STEPS - 1,
            lambda mr, ml, known, _: (
                *neighbours(mr, ml),
                (known, *(apart(known, k * STRIDE) for k in range(1, slabs // STRIDE))),
            ),
            lambda mr, ml, known, tables: (mr, ml, tables),
            mr,
            ml,
            known,
            tables,
        )
        return p, edges, from_left, from_right, tables, totals, *later, now

    p, edges, mr, ml, sums, *tables = first(pltpu.with_memory_space_constraint(populations, pltpu.HBM))
    from_left, from_right = neighbours(mr, ml)
    gathered = lax.all_to_all(sums, "flow", 0, 0)
    totals = jnp.zeros((STEPS, 4), jnp.float32)
    carry = (p, edges, from_left, from_right, tuple(tables), totals, *blocks)
    carry = lax.fori_loop(0, STEPS, step, carry)
    return carry[0], carry[5]


def solution(mesh):
    in_specs = (P(None, "slab", "flow", None), P(), P())
    out_specs = (P(None, "slab", "flow", None), P())
    return jax.shard_map(local, mesh=mesh, in_specs=in_specs, out_specs=out_specs, check_vma=False)
```
